32 devices in a mesh: seq: 2 (over y), fsdp: 16 (over z, x, core).
Axes of the slice: x: 2, y: 2, z: 4, core: 2. Of those that a mesh axis runs over, the one named last changes fastest.
Arguments:
- inputs: bfloat16 [16, 256, 1536], P('fsdp', 'seq'), may hold values from -6 to 6
- positions: int32 [16, 256], P('fsdp', 'seq'), may hold values from 0 to 255, as said below
- segments: int32 [16, 256], P('fsdp'), may hold values from 0 to 3, as said below
- gain_one: float32 [1536], replicated, may hold values from 0.1 to 1.9
- qkv_weight: bfloat16 [1536, 2048], P('fsdp'), may hold values from -0.21875 to 0.21875
- qkv_bias: float32 [2048], replicated, may hold values from -3 to 3
- out_weight: bfloat16 [1536, 1536], P('fsdp'), may hold values from -0.625 to 0.625
- gain_two: float32 [1536], replicated, may hold values from 0.1 to 1.9
- gate_up_weight: bfloat16 [1536, 17920], P('fsdp'), may hold values from -0.15625 to 0.15625
- down_weight: bfloat16 [8960, 1536], P('fsdp'), may hold values from -0.09375 to 0.09375
- cotangent: bfloat16 [16, 256, 1536], P('fsdp', 'seq'), may hold values from -6 to 6
Outputs:
- output: bfloat16 [16, 256, 1536], P('fsdp', 'seq')
- input_grad: float32 [16, 256, 1536], P('fsdp', 'seq')
- gain_one_grad: float32 [1536], replicated
- qkv_weight_grad: float32 [1536, 2048], P('fsdp')
- qkv_bias_grad: float32 [2048], replicated
- out_weight_grad: float32 [1536, 1536], P('fsdp')
- gain_two_grad: float32 [1536], replicated
- gate_up_weight_grad: float32 [1536, 17920], P('fsdp')
- down_weight_grad: float32 [8960, 1536], P('fsdp')
The draws below stay inside these ranges and needn't reach their ends.
Inputs may be any that keep to these rules, and one draw needn't show every extreme that they name: `positions`: the number of earlier tokens of the same segment in the same sequence. `segments`: in each sequence the segment numbers start at 0 at its first token, never fall, and rise by at most one from a token to the next; the first sequence is a single document, every other sequence holds exactly 4 documents.
All inputs are finite; a program needn't handle non-finite values.
Results may differ from the reference program's by a relative error of at most 0.013.
The reference program's roundings to bfloat16 on the way count: a program that leaves them out, or rounds other values in their place, can miss the bound.
Values may be sent and summed in bfloat16 or wider, within the bound.
No kernel may reach another device: no remote copies, remote signals or barrier semaphores. Data moves between devices by JAX's collectives and lax.ppermute only.
A program may use at most 448 MiB of HBM per device.

```python
import jax
import jax.numpy as jnp
from jax import lax

D = 1536
FF = 8960
HQ = 12
KV = 2
HD = 128
LEN = 256
SEQS = 16
QKV = 2048


def pick_starts(row_key):
    return (jax.random.permutation(row_key, LEN - 1)[:3] + 1).astype(jnp.int32)


def document_layout(key):
    base_key = jax.random.fold_in(key, 11)
    row_keys = jax.random.split(base_key, SEQS)
    chosen = jax.vmap(pick_starts)(row_keys)
    token_index = lax.broadcasted_iota(jnp.int32, (SEQS, LEN), 1)
    seq_index = lax.broadcasted_iota(jnp.int32, (SEQS, LEN), 0)
    hit = jnp.any(token_index[:, :, None] == chosen[:, None, :], axis=-1)
    starts = hit & (seq_index > 0) | (token_index == 0)
    segment_ids = jnp.cumsum(starts.astype(jnp.int32), axis=1) - 1
    first_index = lax.cummax(jnp.where(starts, token_index, 0), axis=1)
    return (segment_ids.astype(jnp.int32), (token_index - first_index).astype(jnp.int32))


def draw_segments(key, part):
    return document_layout(key)[0]


def draw_positions(key, part):
    return document_layout(key)[1]


def shard_levels(stream_key, extent, cuts, smallest, largest):
    factor_of, own = 1.0, jax.random.fold_in(stream_key, 6)
    for dim, blocks in cuts:
        steps = jnp.exp(jax.random.uniform(jax.random.fold_in(own, dim), (blocks,), jnp.float32, smallest / len(cuts), largest / len(cuts)))
        factor_of = factor_of * jnp.repeat(steps, extent[dim] // blocks).reshape([-1 if axis == dim else 1 for axis in range(len(extent))])
    return factor_of


def scatter_about(own_key, shape, deviation, bound, cuts=(), kind=jnp.bfloat16):
    level = shard_levels(own_key, shape, cuts, -0.22, 0.18) if cuts else 1.0
    drawn = jax.random.normal(own_key, shape, jnp.float32) * deviation * level
    return jnp.minimum(jnp.maximum(drawn, -bound), bound).astype(kind)


def setup_inputs(seed: int = 0) -> dict:
    keys = jax.random.split(jax.random.key(seed), 12)
    return {
        "inputs": scatter_about(keys[0], (SEQS, LEN, D), 1.0, 6.0, ((0, 16), (1, 2))),
        "positions": draw_positions(jax.random.fold_in(keys[11], 71), 0),
        "segments": draw_segments(jax.random.fold_in(keys[11], 71), 0),
        "gain_one": jnp.clip(1.0 + 0.18 * jax.random.normal(keys[3], (D,), jnp.float32), 0.1, 1.9),
        "qkv_weight": scatter_about(keys[4], (D, QKV), (D // 2) ** -0.5, 0.21875, ((0, 16),)),
        "qkv_bias": scatter_about(keys[5], (QKV,), 0.5, 3.0, (), jnp.float32),
        "out_weight": scatter_about(keys[6], (HQ * HD, D), (HQ * HD // 16) ** -0.5, 0.625, ((0, 16),)),
        "gain_two": jnp.clip(1.0 + 0.18 * jax.random.normal(keys[7], (D,), jnp.float32), 0.1, 1.9),
        "gate_up_weight": scatter_about(keys[8], (D, 2 * FF), D ** -0.5, 0.15625, ((0, 16),)),
        "down_weight": scatter_about(keys[9], (FF, D), (FF // 2) ** -0.5, 0.09375, ((0, 16),)),
        "cotangent": scatter_about(keys[10], (SEQS, LEN, D), 1.0, 6.0, ((0, 16), (1, 2))),
    }


@jax.custom_vjp
def low(v):
    return lax.optimization_barrier(v.astype(jnp.bfloat16)).astype(jnp.float32)

@jax.custom_vjp
def low_back(v):
    return v

def low_keep(v):
    return (low(v), None)

def low_pass(kept, grad):
    return (grad,)

def back_keep(v):
    return (v, None)

def back_low(kept, grad):
    return (low(grad),)
low.defvjp(low_keep, low_pass)
low_back.defvjp(back_keep, back_low)
rope_base = 1000000.0
norm_eps = 1e-06
highest = lax.Precision.HIGHEST

def rope_angles(positions):
    steps_half = jnp.arange(HD // 2, dtype=jnp.float32)
    inverse = rope_base ** (-2.0 * steps_half / HD)
    angles = positions.astype(jnp.float32)[..., None] * inverse
    return (jnp.cos(angles), jnp.sin(angles))

def rotate(values, cosines, sines):
    half_size = values.shape[-1] // 2
    front_half = values[..., :half_size]
    back_half = values[..., half_size:]
    cos_heads = cosines[..., None, :]
    sin_heads = sines[..., None, :]
    return jnp.concatenate([front_half * cos_heads - back_half * sin_heads, back_half * cos_heads + front_half * sin_heads], axis=-1)

def rms_scale(values):
    return lax.rsqrt(lax.optimization_barrier(jnp.mean(values * values, axis=-1, keepdims=True)) + norm_eps)

def attend(queries, key_rows, value_rows, segment):
    length = queries.shape[0]
    grouped = queries.reshape(length, KV, HQ // KV, HD)
    scores = jnp.einsum('lgqd,mgd->gqlm', grouped, key_rows, precision=highest) * HD ** (-0.5)
    scores = low_back(scores)
    row_index = jnp.arange(length)[:, None]
    col_index = jnp.arange(length)[None, :]
    allowed = (row_index >= col_index) & (segment[:, None] == segment[None, :])
    scores = jnp.where(allowed, scores, -1e+30)
    weights = low(jax.nn.softmax(scores, axis=-1))
    attended = jnp.einsum('gqlm,mgd->lgqd', weights, value_rows, precision=highest)
    return attended.reshape(length, HQ, HD)

def attend_packed(packed):
    return attend(packed[0], packed[1], packed[2], packed[3])

def layer(block_in, gain_one, qkv_weight, qkv_bias, out_weight, gain_two, gate_up_weight, down_weight, cosines, sines, segment):
    members = block_in.shape[0]
    query_width = HQ * HD
    key_width = KV * HD
    residual_in = block_in.reshape(members * LEN, D)
    normed = low(residual_in * rms_scale(residual_in) * gain_one)
    projected = low_back(jnp.dot(normed, qkv_weight, precision=highest) + qkv_bias)
    queries = projected[:, :query_width].reshape(members, LEN, HQ, HD)
    key_rows = projected[:, query_width:query_width + key_width].reshape(members, LEN, KV, HD)
    value_rows = projected[:, query_width + key_width:].reshape(members, LEN, KV, HD)
    queries = low_back(low(rotate(queries, cosines, sines)))
    key_rows = low_back(low(rotate(key_rows, cosines, sines)))
    value_rows = low_back(low(value_rows))
    attended = lax.map(jax.checkpoint(attend_packed), (queries, key_rows, value_rows, segment))
    attended = low_back(low(attended.reshape(members * LEN, query_width)))
    branch = low_back(jnp.dot(attended, out_weight, precision=highest))
    middle = residual_in + branch
    normed_two = low(middle * rms_scale(middle) * gain_two)
    gate_up = low_back(jnp.dot(normed_two, gate_up_weight, precision=highest))
    hidden = low(jax.nn.silu(gate_up[:, :FF]) * gate_up[:, FF:])
    result = middle + jnp.dot(hidden, down_weight, precision=highest)
    return result.reshape(members, LEN, D)

def reference(inputs, positions, segments, gain_one, qkv_weight, qkv_bias, out_weight, gain_two, gate_up_weight, down_weight, cotangent):
    grouping = 1
    while grouping * 2 * LEN <= 4096 and SEQS % (grouping * 2) == 0:
        grouping = grouping * 2
    blocks = SEQS // grouping
    cosines, sines = rope_angles(positions)
    params = (gain_one.astype(jnp.float32), qkv_weight.astype(jnp.float32), qkv_bias.astype(jnp.float32), out_weight.astype(jnp.float32), gain_two.astype(jnp.float32), gate_up_weight.astype(jnp.float32), down_weight.astype(jnp.float32))
    stacked = (inputs.reshape(blocks, grouping, LEN, D), cosines.reshape(blocks, grouping, LEN, HD // 2), sines.reshape(blocks, grouping, LEN, HD // 2), segments.reshape(blocks, grouping, LEN), cotangent.reshape(blocks, grouping, LEN, D))

    def one_group(totals, pieces):
        block_in, block_cos, block_sin, block_seg, block_cot = pieces

        def forward(values_in, gain_a, weight_a, bias_a, weight_b, gain_b, weight_c, weight_d):
            return layer(values_in, gain_a, weight_a, bias_a, weight_b, gain_b, weight_c, weight_d, block_cos, block_sin, block_seg)
        result, backward = jax.vjp(forward, block_in.astype(jnp.float32), params[0], params[1], params[2], params[3], params[4], params[5], params[6])
        grads = backward(block_cot.astype(jnp.float32))
        totals = tuple((total + grad for total, grad in zip(totals, grads[1:])))
        return (totals, (result.astype(jnp.bfloat16), grads[0]))
    zeros = tuple((jnp.zeros_like(param) for param in params))
    totals, (outputs, input_grads) = lax.scan(one_group, zeros, stacked)
    return (outputs.reshape(SEQS, LEN, D), input_grads.reshape(SEQS, LEN, D), totals[0], totals[1], totals[2], totals[3], totals[4], totals[5], totals[6])
```

```python
import functools

import jax
import jax.numpy as jnp
from jax import lax
from jax.experimental import pallas as pl
from jax.experimental.pallas import tpu as pltpu
from jax.sharding import PartitionSpec as P

D = 1536
FF = 8960
HQ = 12
KV = 2
HD = 128
GROUP = HQ // KV
QW = HQ * HD
KW = KV * HD

rope_base = 1000000.0
norm_eps = 1e-06
bf16 = jnp.bfloat16
f32 = jnp.float32


def flip(value, k):
    size = lax.axis_size("fsdp")
    return lax.ppermute(value, "fsdp", [(i, i ^ k) for i in range(size)])


def swap(value):
    return lax.ppermute(value, "seq", [(0, 1), (1, 0)])


def add(left, right):
    return left.astype(f32) + right.astype(f32)


def dot(left, right):
    return jnp.dot(left, right, preferred_element_type=f32)


def dot_t(left, right):
    return lax.dot_general(left, right, (((1,), (1,)), ((), ())), preferred_element_type=f32)


def t_dot(left, right):
    return lax.dot_general(left, right, (((0,), (0,)), ((), ())), preferred_element_type=f32)


def gather_tokens(rows):
    blocks = []
    for dz in range(lax.axis_size("fsdp") // 4):
        own = flip(rows, 4 * dz) if dz else rows
        pair = jnp.concatenate([own, flip(own, 2)], axis=0)
        blocks.append(jnp.concatenate([pair, flip(pair, 1)], axis=0))
    return blocks


def scatter_tokens(near, far, dz):
    tokens = near.shape[0] // 2
    both = add(near, flip(far, 1))
    mine = add(both[:tokens], flip(both[tokens:].astype(bf16), 2))
    return flip(mine.astype(bf16), 4 * dz) if dz else mine


def place_kernel(count, where, *refs):
    out = refs[-1]
    at = 0
    for ref in refs[:-1]:
        for i in range(ref.shape[0]):
            out[where[at]] = ref[i]
            at += 1


def place_blocks(pieces, where):
    count = sum(p.shape[0] for p in pieces)
    shape = (count,) + pieces[0].shape[1:]
    return pl.pallas_call(
        functools.partial(place_kernel, count),
        out_shape=jax.ShapeDtypeStruct(shape, pieces[0].dtype),
        in_specs=[pl.BlockSpec(memory_space=pltpu.SMEM)]
        + [pl.BlockSpec(memory_space=pltpu.VMEM)] * len(pieces),
        out_specs=pl.BlockSpec(memory_space=pltpu.VMEM),
        compiler_params=pltpu.CompilerParams(vmem_limit_bytes=40 * 1024 * 1024),
    )(where, *pieces)


def gather_weight(shard, me, s):
    size = lax.axis_size("fsdp")
    half = shard.shape[0] // 2
    own = lax.dynamic_slice_in_dim(shard, s * half, half, axis=0)
    pieces, where = [], []
    for dz in range(size // 4):
        first = flip(own, 4 * dz) if dz else own
        pair = jnp.stack([first, flip(first, 2)])
        four = jnp.concatenate([pair, swap(pair)], axis=0)
        pieces += [four, flip(four, 1)]
        for dc in range(2):
            for h in range(2):
                for dx in range(2):
                    where.append((me ^ (4 * dz + 2 * dx + dc)) * 2 + (s ^ h))
    placed = place_blocks(pieces, jnp.stack(where).astype(jnp.int32))
    return placed.reshape(size * 2 * half, shard.shape[1])


def scatter_weight(left, right, me, s):
    size = lax.axis_size("fsdp")
    steps = size // 4
    width = left.shape[1]
    half = width // size // 2
    turned = left.T.reshape(size * 2, half, left.shape[0])
    where = []
    for place in range(size):
        for h in range(2):
            k = me ^ place
            dz, dx, dc = k // 4, (k // 2) % 2, k % 2
            where.append(((dc * 2 + dx) * 2 + (s ^ h)) * steps + dz)
    turned = place_blocks([turned], jnp.stack(where).astype(jnp.int32)).reshape(
        2, width // 2, left.shape[0]
    )
    far = flip(dot(turned[1], right).astype(bf16), 1)
    total = add(dot(turned[0], right), far)
    quarter = width // 4
    total = add(total[:quarter], flip(total[quarter:].astype(bf16), 2))
    eighth = width // 8
    total = add(total[:eighth], swap(total[eighth:].astype(bf16)))
    mine = total[:half]
    for dz in range(1, steps):
        mine = add(mine, flip(total[dz * half : (dz + 1) * half].astype(bf16), 4 * dz))
    return join_halves(mine.astype(bf16), s)


def join_halves(mine, s):
    other = swap(mine)
    low = jnp.where(s == 0, mine, other)
    high = jnp.where(s == 0, other, mine)
    return jnp.concatenate([low, high], axis=0).astype(f32)


def sum_everywhere(value):
    bit = 1
    while bit < lax.axis_size("fsdp"):
        value = value + flip(value, bit)
        bit *= 2
    return value + swap(value)


def rope_angles(positions):
    steps_half = jnp.arange(HD // 2, dtype=f32)
    inverse = rope_base ** (-2.0 * steps_half / HD)
    angles = positions.astype(f32)[..., None] * inverse
    return (jnp.cos(angles), jnp.sin(angles))


def rotate(values, cosines, sines):
    half_size = values.shape[-1] // 2
    front_half = values[..., :half_size]
    back_half = values[..., half_size:]
    cos_heads = cosines[..., None, :]
    sin_heads = sines[..., None, :]
    return jnp.concatenate(
        [
            front_half * cos_heads - back_half * sin_heads,
            back_half * cos_heads + front_half * sin_heads,
        ],
        axis=-1,
    )


def rms_scale(values):
    return lax.rsqrt(jnp.mean(values * values, axis=-1, keepdims=True) + norm_eps)


def norm_backward(grad_normed, values, scale_rows, gain):
    scaled = grad_normed * gain
    gain_part = jnp.sum(grad_normed * values * scale_rows, axis=0)
    grad_values = scale_rows * scaled - values * scale_rows**3 * jnp.mean(
        scaled * values, axis=-1, keepdims=True
    )
    return (grad_values, gain_part)


def attention_probs(queries, keys, allowed):
    tokens = queries.shape[0]
    grouped = queries.reshape(tokens, KV, GROUP, HD)
    scores = jnp.einsum("tgqd,sgd->gqts", grouped, keys, preferred_element_type=f32) * HD ** (-0.5)
    scores = jnp.where(allowed, scores, -1e30)
    peak = jnp.max(scores, axis=-1, keepdims=True)
    weights = jnp.exp(scores - peak)
    return weights / jnp.sum(weights, axis=-1, keepdims=True)


def attend_forward(probs, values):
    tokens = probs.shape[2]
    out = jnp.einsum("gqts,sgd->tgqd", probs.astype(bf16), values, preferred_element_type=f32)
    return out.reshape(tokens, QW).astype(bf16)


def attend_backward(queries, keys, values, probs, grad_out):
    tokens = queries.shape[0]
    grouped = queries.reshape(tokens, KV, GROUP, HD)
    grad_grouped = grad_out.reshape(tokens, KV, GROUP, HD)
    grad_probs = jnp.einsum("tgqd,sgd->gqts", grad_grouped, values, preferred_element_type=f32)
    grad_values = jnp.einsum(
        "gqts,tgqd->sgd", probs.astype(bf16), grad_grouped, preferred_element_type=f32
    )
    balance = jnp.sum(probs * grad_probs, axis=-1, keepdims=True)
    grad_scores = (probs * (grad_probs - balance)).astype(bf16)
    factor = HD ** (-0.5)
    grad_queries = (
        jnp.einsum("gqts,sgd->tgqd", grad_scores, keys, preferred_element_type=f32) * factor
    )
    grad_keys = (
        jnp.einsum("gqts,tgqd->sgd", grad_scores, grouped, preferred_element_type=f32) * factor
    )
    return (grad_queries.reshape(tokens, HQ, HD), grad_keys, grad_values)


def shuffle_gate_up(shard, me, s):
    size = lax.axis_size("fsdp")
    half = shard.shape[0] // 2
    unit = FF // size
    own = lax.dynamic_slice_in_dim(shard, s * half, half, axis=0)
    blocks = jnp.transpose(own.reshape(half, 2, size, unit), (2, 0, 1, 3)).reshape(
        size, half, 2 * unit
    )
    pieces = [lax.dynamic_index_in_dim(blocks, me, 0)]
    where = [me]
    for k in range(1, size):
        pieces.append(flip(lax.dynamic_index_in_dim(blocks, me ^ k, 0), k))
        where.append(me ^ k)
    mine = place_blocks(pieces, jnp.stack(where).astype(jnp.int32))
    other = swap(mine)
    low = jnp.where(s == 0, mine, other)
    high = jnp.where(s == 0, other, mine)
    whole = jnp.stack([low, high], axis=1).reshape(size * 2 * half, 2, unit)
    padded = -(-unit // 128) * 128
    whole = jnp.pad(whole, ((0, 0), (0, 0), (0, padded - unit)))
    return whole.reshape(size * 2 * half, 2 * padded)


def unshuffle_gate_up(grad, me, s):
    size = lax.axis_size("fsdp")
    unit = FF // size
    padded = grad.shape[1] // 2
    half = grad.shape[0] // size // 2
    grad = jnp.concatenate([grad[:, :unit], grad[:, padded : padded + unit]], axis=1)
    parts = grad.reshape(size, 2, half, 2 * unit)
    keep = lax.dynamic_index_in_dim(parts, s, 1, keepdims=False)
    give = lax.dynamic_index_in_dim(parts, 1 - s, 1, keepdims=False).astype(bf16)
    total = add(keep, swap(give)).astype(bf16)
    pieces = [lax.dynamic_index_in_dim(total, me, 0)]
    where = [me]
    for k in range(1, size):
        pieces.append(flip(lax.dynamic_index_in_dim(total, me ^ k, 0), k))
        where.append(me ^ k)
    mine = place_blocks(pieces, jnp.stack(where).astype(jnp.int32))
    mine = jnp.transpose(mine.reshape(size, half, 2, unit), (1, 2, 0, 3)).reshape(half, 2 * FF)
    return join_halves(mine, s)


def body(
    inputs,
    positions,
    segments,
    gain_one,
    qkv_weight,
    qkv_bias,
    out_weight,
    gain_two,
    gate_up_weight,
    down_weight,
    cotangent,
):
    tokens = inputs.shape[0] * inputs.shape[1]
    size = lax.axis_size("fsdp")
    steps = size // 4
    me = lax.axis_index("fsdp")
    s = lax.axis_index("seq")
    unit = FF // size
    padded = -(-unit // 128) * 128

    qkv_full = gather_weight(qkv_weight, me, s)
    out_full = gather_weight(out_weight, me, s)
    gate_up_full = shuffle_gate_up(gate_up_weight, me, s)
    down_full = jnp.pad(down_weight, ((0, padded - unit), (0, 0)))
    grad_rows = cotangent.reshape(tokens, D)
    cot_blocks = gather_tokens(grad_rows)

    residual_in = inputs.reshape(tokens, D).astype(f32)
    cosines, sines = rope_angles(positions.reshape(tokens))
    scale_one = rms_scale(residual_in)
    normed = (residual_in * scale_one * gain_one).astype(bf16)
    projected = dot(normed, qkv_full) + qkv_bias
    queries = rotate(projected[:, :QW].reshape(tokens, HQ, HD), cosines, sines).astype(bf16)
    key_rows = rotate(projected[:, QW : QW + KW].reshape(tokens, KV, HD), cosines, sines)
    mine_kv = jnp.concatenate(
        [key_rows.astype(bf16).reshape(tokens, KW), projected[:, QW + KW :].astype(bf16)], axis=1
    )
    all_kv = jnp.concatenate([mine_kv, swap(mine_kv)], axis=0)
    keys = all_kv[:, :KW].reshape(2 * tokens, KV, HD)
    values = all_kv[:, KW:].reshape(2 * tokens, KV, HD)
    ids = segments.reshape(2, tokens)
    mine_ids = lax.dynamic_index_in_dim(ids, s, 0, keepdims=False)
    other_ids = lax.dynamic_index_in_dim(ids, 1 - s, 0, keepdims=False)
    row_index = lax.broadcasted_iota(jnp.int32, (tokens, tokens), 0)
    col_index = lax.broadcasted_iota(jnp.int32, (tokens, tokens), 1)
    near = (mine_ids[:, None] == mine_ids[None, :]) & (row_index >= col_index)
    far = (mine_ids[:, None] == other_ids[None, :]) & (s == 1)
    allowed = jnp.concatenate([near, far], axis=1)[None, None]
    probs = attention_probs(queries, keys, allowed)
    attended = attend_forward(probs, values)
    middle = residual_in + dot(attended, out_full)
    scale_two = rms_scale(middle)
    normed_two = (middle * scale_two * gain_two).astype(bf16)

    token_blocks = gather_tokens(normed_two)
    hidden_blocks, grad_blocks = [], []
    back_total, out_total = [], []
    for dz in range(steps):
        gate_up = dot(token_blocks[dz], gate_up_full)
        gate, up_part = gate_up[:, :padded], gate_up[:, padded:]
        sigmoid_gate = jax.nn.sigmoid(gate)
        silu_gate = gate * sigmoid_gate
        hidden = (silu_gate * up_part).astype(bf16)
        grad_hidden = dot_t(cot_blocks[dz], down_full)
        grad_gate = grad_hidden * up_part * sigmoid_gate * (1.0 + gate * (1.0 - sigmoid_gate))
        grad_up = grad_hidden * silu_gate
        grad_gate_up = jnp.concatenate([grad_gate, grad_up], axis=1).astype(bf16)
        hidden_blocks.append(hidden)
        grad_blocks.append(grad_gate_up)
        low = 2 * tokens
        back_far = dot_t(grad_gate_up[low:], gate_up_full).astype(bf16)
        back_near = dot_t(grad_gate_up[:low], gate_up_full)
        back_total.append(scatter_tokens(back_near, back_far, dz))
        out_far = dot(hidden[low:], down_full).astype(bf16)
        out_near = dot(hidden[:low], down_full)
        out_total.append(scatter_tokens(out_near, out_far, dz))
    grad_normed_two = functools.reduce(add, back_total)
    result = middle + functools.reduce(add, out_total)
    output = result.astype(bf16).reshape(inputs.shape)

    hidden_all = jnp.concatenate(hidden_blocks, axis=0)
    grad_all = jnp.concatenate(grad_blocks, axis=0)
    cot_all = jnp.concatenate(cot_blocks, axis=0)
    tokens_all = jnp.concatenate(token_blocks, axis=0)
    gate_up_part = t_dot(tokens_all, grad_all)
    down_part = t_dot(hidden_all, cot_all)[:unit].astype(bf16)
    gate_up_total = unshuffle_gate_up(gate_up_part, me, s)
    down_total = add(down_part, swap(down_part))

    grad_norm_two, gain_two_part = norm_backward(grad_normed_two, middle, scale_two, gain_two)
    grad_middle = grad_rows.astype(f32) + grad_norm_two
    grad_branch = grad_middle.astype(bf16)
    grad_attended = dot_t(grad_branch, out_full).astype(bf16)
    out_weight_total = scatter_weight(attended, grad_branch, me, s)
    grad_q, grad_k, grad_v = attend_backward(queries, keys, values, probs, grad_attended)
    give = jnp.concatenate(
        [grad_k[tokens:].reshape(tokens, KW), grad_v[tokens:].reshape(tokens, KW)], axis=1
    )
    keep = jnp.concatenate(
        [grad_k[:tokens].reshape(tokens, KW), grad_v[:tokens].reshape(tokens, KW)], axis=1
    )
    grad_kv = add(keep, swap(give.astype(bf16))).astype(bf16)
    grad_q = rotate(grad_q.astype(bf16).astype(f32), cosines, -sines).reshape(tokens, QW)
    grad_k = rotate(
        grad_kv[:, :KW].astype(f32).reshape(tokens, KV, HD), cosines, -sines
    ).reshape(tokens, KW)
    grad_projected = jnp.concatenate(
        [grad_q.astype(bf16), grad_k.astype(bf16), grad_kv[:, KW:]], axis=1
    )
    bias_part = jnp.sum(grad_projected.astype(f32), axis=0)
    grad_normed = dot_t(grad_projected, qkv_full)
    qkv_weight_total = scatter_weight(normed, grad_projected, me, s)
    grad_norm_one, gain_one_part = norm_backward(grad_normed, residual_in, scale_one, gain_one)
    input_grad = (grad_middle + grad_norm_one).reshape(inputs.shape)
    sums = sum_everywhere(jnp.concatenate([gain_one_part, bias_part, gain_two_part]))
    width = bias_part.shape[0]
    return (
        output,
        input_grad,
        sums[:D],
        qkv_weight_total,
        sums[D : D + width],
        out_weight_total,
        sums[D + width :],
        gate_up_total,
        down_total,
    )


def solution(mesh):
    placed = (
        P("fsdp", "seq", None),
        P("fsdp", "seq"),
        P("fsdp", None),
        P(),
        P("fsdp", None),
        P(),
        P("fsdp", None),
        P(),
        P("fsdp", None),
        P("fsdp", None),
        P("fsdp", "seq", None),
    )
    return jax.shard_map(
        body,
        mesh=mesh,
        in_specs=placed,
        out_specs=(
            P("fsdp", "seq", None),
            P("fsdp", "seq", None),
            P(),
            P("fsdp", None),
            P(),
            P("fsdp", None),
            P(),
            P("fsdp", None),
            P("fsdp", None),
        ),
        check_vma=False,
    )
```

```python
import functools

import jax
import jax.numpy as jnp
from jax import lax
from jax.experimental import pallas as pl
from jax.experimental.pallas import tpu as pltpu
from jax.sharding import PartitionSpec as P

D = 1536
FF = 8960
HQ = 12
KV = 2
HD = 128
GROUP = HQ // KV
QW = HQ * HD
KW = KV * HD

rope_base = 1000000.0
norm_eps = 1e-06
bf16 = jnp.bfloat16
f32 = jnp.float32


CORE, X, Z = 1, 2, 4
ROTATED = ((Z, X, "y"), (X, "y", Z), ("y", Z, X))
CROSSED = ((X, Z), (Z, X))
VMEM = 48 * 1024 * 1024


def far_bits():
    return [bit for bit in (8 << i for i in range(16)) if bit < lax.axis_size("fsdp")]


def after(value, *earlier):
    return lax.optimization_barrier((value,) + earlier)[0]


class Move:
    def __init__(self, steps):
        self.steps = steps
        self.result = self.arrived = None
        self.wanted = next(steps)

    def resume(self, beside=()):
        if self.arrived is None:
            return
        arrived, self.arrived = self.arrived, None
        if beside:
            arrived = [after(value, *beside) for value in arrived]
        try:
            self.wanted = self.steps.send(arrived)
        except StopIteration as stop:
            self.result = stop.value


class Lanes:
    def __init__(self):
        self.moves, self.flying, self.ended, self.before, self.kernels = [], [], [], [], []

    def round(self, *entries):
        for move in self.moves:
            move.resume(self.kernels)
        self.moves = []
        ended = [value for value, left in self.flying if left <= 1] + self.kernels
        self.before, self.ended = ended + self.ended, ended
        self.flying = [(value, left - 1) for value, left in self.flying if left > 1]
        self.kernels = []
        self.more(*entries)

    def more(self, *entries):
        size = lax.axis_size("fsdp")
        for entry in entries:
            move, lasts = entry if isinstance(entry, tuple) else (entry, 1)
            if not move.wanted:
                continue
            move.arrived = []
            for link, value in move.wanted:
                if self.before:
                    value = after(value, *self.before)
                if link == "y":
                    value = lax.ppermute(value, "seq", [(0, 1), (1, 0)])
                else:
                    value = lax.ppermute(value, "fsdp", [(i, i ^ link) for i in range(size)])
                move.arrived.append(value)
                self.flying.append((value, lasts))
            move.wanted = None
            self.moves.append(move)

    def hold(self, value):
        return after(value, *self.before) if self.before else value

    def beside(self, *values):
        self.kernels += values

    def drain(self, *moves):
        for move in moves:
            move.resume()
        while any(move.wanted for move in moves):
            self.round(*moves)
            for move in moves:
                move.resume()
        return [move.result for move in moves]


def add(left, right):
    return left.astype(f32) + right.astype(f32)


def dot(left, right):
    return jnp.dot(left, right, preferred_element_type=f32)


def dot_t(left, right):
    return lax.dot_general(left, right, (((1,), (1,)), ((), ())), preferred_element_type=f32)


def t_dot(left, right):
    return lax.dot_general(left, right, (((0,), (0,)), ((), ())), preferred_element_type=f32)


def join(*pieces, axis=0):
    return jnp.concatenate(pieces, axis=axis)


def pick(value, index, axis):
    return lax.index_in_dim(value, index, axis, keepdims=False)


def whole_call(kernel, out_shape, scalars, arrays, scratch=(), flops=0):
    outs = out_shape if isinstance(out_shape, (list, tuple)) else [out_shape]
    moved = sum(a.size * a.dtype.itemsize for a in list(arrays) + list(outs))
    spec = pl.BlockSpec(memory_space=pltpu.VMEM)
    return pl.pallas_call(
        kernel,
        out_shape=out_shape,
        in_specs=[pl.BlockSpec(memory_space=pltpu.SMEM)] + [spec] * len(arrays),
        out_specs=jax.tree.map(lambda _: spec, out_shape),
        scratch_shapes=list(scratch),
        compiler_params=pltpu.CompilerParams(vmem_limit_bytes=VMEM),
        cost_estimate=pl.CostEstimate(flops=flops, bytes_accessed=moved, transcendentals=0),
    )(jnp.stack(scalars).astype(jnp.int32), *arrays)


def gather_tokens(rows, blocks):
    state = rows[None]
    for bit in far_bits():
        (got,) = yield [(bit, state)]
        state = join(state, got)
    half, width = rows.shape[0] // 2, rows.shape[1]
    first, second = state[:, :half], state[:, half:]
    got = yield [(Z, first), (X, second)]
    first, second = join(first, got[0]), join(second, got[1])
    blocks.append([v.reshape(-1, width) for v in (first, second)])
    last = yield [(X, first), (Z, second)]
    blocks.append([v.reshape(-1, width) for v in last])


def scatter_tokens(early, last):
    width = last[0].shape[1]
    far = far_bits()
    count = 1 << len(far)
    half = last[0].shape[0] // count // 2
    got = yield [(X, last[0]), (Z, last[1])]
    first = add(early[0], got[0]).reshape(2, count, half, width)
    second = add(early[1], got[1]).reshape(2, count, half, width)
    got = yield [(Z, first[1].astype(bf16)), (X, second[1].astype(bf16))]
    state = join(add(first[0], got[0]), add(second[0], got[1]), axis=1)
    for bit in reversed(far):
        count //= 2
        (got,) = yield [(bit, state[count:].astype(bf16))]
        state = add(state[:count], got)
    return state[0]


def place_kernel(where, *refs):
    out = refs[-1]
    at = 0
    for ref in refs[:-1]:
        for i in range(ref.shape[0]):
            out[where[at]] = ref[i]
            at += 1


def cut_columns(width):
    third = width // 3 // 128 * 128
    return ((0, third), (third, 2 * third), (2 * third, width))


def gather_weight(shard, me, s):
    size = lax.axis_size("fsdp")
    half, width = shard.shape[0] // 2, shard.shape[1]
    state = lax.dynamic_index_in_dim(shard.reshape(2, half, width), s, 0)
    marks = [(0, 0)]
    for bit in far_bits():
        (got,) = yield [(bit, state)]
        state = join(state, got)
        marks = marks + [(f ^ bit, h) for f, h in marks]
    states = [state[:, :, low:high] for low, high in cut_columns(width)]
    for step in range(3):
        got = yield [(ROTATED[part][step], states[part]) for part in range(3)]
        states = [join(*pair) for pair in zip(states, got)]
    turns = []
    for order in ROTATED:
        index = [order.index(link) for link in reversed(ROTATED[0])]
        turns.append([2 - i for i in index])
    count = len(marks)
    split = [v.reshape(2, 2, 2, count, half, v.shape[-1]) for v in states]
    state = join(*[jnp.transpose(v, t + [3, 4, 5]) for v, t in zip(split, turns)], axis=-1)
    state = state.reshape(8 * count, half, width)
    for link in ROTATED[0]:
        marks = marks + [(f, 1 - h) if link == "y" else (f ^ link, h) for f, h in marks]
    (got,) = yield [(CORE, state)]
    where = []
    for core in range(2):
        where += [(me ^ f ^ core) * 2 + (s ^ h) for f, h in marks]
    whole = whole_call(
        place_kernel,
        jax.ShapeDtypeStruct((size * 2, half, width), bf16),
        where,
        [state, got],
    )
    return whole.reshape(size * 2 * half, width)


def gather_weight_plain(shard, me):
    size = lax.axis_size("fsdp")
    rows, width = shard.shape
    state = shard[None]
    marks = [0]
    for bit in far_bits():
        (got,) = yield [(bit, state)]
        state = join(state, got)
        marks = marks + [f ^ bit for f in marks]
    half = width // 2
    first, second = state[:, :, :half], state[:, :, half:]
    got = yield [(X, first), (Z, second)]
    first, second = join(first, got[0]), join(second, got[1])
    got = yield [(Z, first), (X, second)]
    count = len(marks)
    second = join(second[:count], got[1][:count], second[count:], got[1][count:])
    state = join(join(first, got[0]), second, axis=2)
    for link in (X, Z):
        marks = marks + [f ^ link for f in marks]
    (got,) = yield [(CORE, state)]
    where = [me ^ f for f in marks] + [me ^ f ^ CORE for f in marks]
    whole = whole_call(
        place_kernel, jax.ShapeDtypeStruct((size, rows, width), bf16), where, [state, got]
    )
    return whole.reshape(size * rows, width)


def order_kernel(where, source, out):
    for i in range(source.shape[0]):
        out[where[i]] = source[i]


def scatter_weight(left, right, me, s):
    size = lax.axis_size("fsdp")
    far = far_bits()
    count = 1 << len(far)
    rows, width = left.shape[1], right.shape[1]
    half = rows // size // 2
    turned = left.T.reshape(size * 2, half, left.shape[0])
    where = []
    for place in range(size):
        for h in range(2):
            k = me ^ place
            kept = ((k % 2) * 2 + (k // 2) % 2) * 2 + (k // 4) % 2
            where.append((kept * count + k // 8) * 2 + (s ^ h))
    turned = whole_call(
        order_kernel, jax.ShapeDtypeStruct(turned.shape, bf16), where, [turned]
    ).reshape(2, rows // 2, left.shape[0])
    (got,) = yield [(CORE, dot(turned[1], right).astype(bf16))]
    total = add(dot(turned[0], right), got).reshape(2, 2, count, 2, half, width)
    low, high = total[..., : width // 2], total[..., width // 2 :]
    got = yield [(X, low[1].astype(bf16)), (Z, high[:, 1].astype(bf16))]
    low, high = add(low[0], got[0]), add(high[:, 0], got[1])
    got = yield [(Z, low[1].astype(bf16)), (X, high[1].astype(bf16))]
    state = join(add(low[0], got[0]), add(high[0], got[1]), axis=-1)
    for bit in reversed(far):
        count //= 2
        (got,) = yield [(bit, state[count:].astype(bf16))]
        state = add(state[:count], got)
    (got,) = yield [("y", state[0, 1].astype(bf16))]
    mine = add(state[0, 0], got).astype(bf16)
    (other,) = yield [("y", mine)]
    low = jnp.where(s == 0, mine, other)
    high = jnp.where(s == 0, other, mine)
    return join(low, high).astype(f32)


def sum_everywhere(value):
    for link in [CORE, X, Z] + far_bits() + ["y"]:
        (got,) = yield [(link, value)]
        value = value + got
    return value


def swap(link, value):
    (got,) = yield [(link, value)]
    return got


def exchange_blocks(blocks, order):
    axes = list(reversed(far_bits())) + [Z, X]
    state = blocks.reshape((1,) + (2,) * len(axes) + blocks.shape[1:])
    marks = [0]
    for link in order:
        axis = 1 + axes.index(link)
        axes.remove(link)
        (got,) = yield [(link, pick(state, 1, axis))]
        state = join(pick(state, 0, axis), got)
        marks = marks + [f ^ link for f in marks]
    return state, marks


def split_kernel(unit, at, shard, gate, up):
    for chip in range(gate.shape[0]):
        low = chip * unit
        gate[at[0] ^ chip] = shard[at[1], :, low : low + unit]
        up[at[0] ^ chip] = shard[at[1], :, FF + low : FF + low + unit]


def weave_kernel(unit, where, *refs):
    out = refs[-1]
    half, padded = out.shape[1], out.shape[2] // 2
    at = 0
    for part in range(2):
        low = part * padded
        for ref in refs[3 * part : 3 * part + 3]:
            for i in range(ref.shape[0]):
                out[where[at], :, low : low + unit] = ref[i]
                if padded > unit:
                    out[where[at], :, low + unit : low + padded] = jnp.zeros(
                        (half, padded - unit), out.dtype
                    )
                at += 1


def split_gate_up(shard, me, s):
    size = lax.axis_size("fsdp")
    half = shard.shape[0] // 2
    unit = 2 * FF // size
    block = jax.ShapeDtypeStruct((size // 2, half, unit), bf16)
    return whole_call(
        functools.partial(split_kernel, unit),
        (block, block),
        [me // 2, s],
        [shard.reshape(2, half, 2 * FF)],
    )


def shuffle_part(blocks, order):
    mine, marks = yield from exchange_blocks(blocks, order)
    (other,) = yield [("y", mine)]
    (got,) = yield [(CORE, join(mine, other))]
    return [mine, other, got], marks


def weave_gate_up(parts, me, s):
    size = lax.axis_size("fsdp")
    half, unit = parts[0][0][0].shape[1:]
    padded = -(-unit // 384) * 384
    pieces, where = [], []
    for blocks, marks in parts:
        pieces += blocks
        for core in range(2):
            for h in range(2):
                where += [(me ^ f ^ core) * 2 + (s ^ h) for f in marks]
    whole = whole_call(
        functools.partial(weave_kernel, unit),
        jax.ShapeDtypeStruct((size * 2, half, 2 * padded), bf16),
        where,
        pieces,
    )
    return whole.reshape(size * 2 * half, 2 * padded)


def grad_kernel(count, unit, at, *refs):
    outs = refs[-2:]
    half = outs[0].shape[2]
    total = 0.0
    for j in range(count):
        total = total + t_dot(refs[j][...], refs[count + j][...])
    total = total.astype(bf16)[:, :unit]
    here = total.shape[0] // (2 * half)
    for i in range(here):
        k = at[0] ^ (pl.program_id(0) * here + i)
        for h in range(2):
            low = (2 * i + h) * half
            for core, out in enumerate(outs):

                @pl.when(k % 2 == core)
                def _():
                    out[at[1] ^ h, k // 2] = total[low : low + half]


def gate_up_grad(token_blocks, grad_blocks, me, s):
    size = lax.axis_size("fsdp")
    unit = 2 * FF // size
    padded = grad_blocks[0].shape[1]
    half = D // size // 2
    count = len(token_blocks)
    rows = token_blocks[0].shape[0]
    tile = 768
    return pl.pallas_call(
        functools.partial(grad_kernel, count, unit),
        out_shape=[jax.ShapeDtypeStruct((2, size // 2, half, unit), bf16)] * 2,
        grid=(D // tile,),
        in_specs=[pl.BlockSpec(memory_space=pltpu.SMEM)]
        + [pl.BlockSpec((rows, tile), lambda i: (0, i))] * count
        + [pl.BlockSpec((rows, padded), lambda i: (0, 0))] * count,
        out_specs=[pl.BlockSpec(memory_space=pltpu.VMEM)] * 2,
        compiler_params=pltpu.CompilerParams(vmem_limit_bytes=VMEM),
        cost_estimate=pl.CostEstimate(
            flops=2 * count * rows * D * padded,
            bytes_accessed=2 * count * rows * (D + padded) + 4 * D * unit,
            transcendentals=0,
        ),
    )(jnp.stack([me, s]).astype(jnp.int32), *token_blocks, *grad_blocks)


def spread_kernel(unit, where, blocks, out, held):
    for i in range(blocks.shape[0]):
        held[where[i]] = blocks[i]
    for chip in range(blocks.shape[0]):
        out[:, chip * unit : (chip + 1) * unit] = held[chip]


def widen_kernel(at, gate, up, other_gate, other_up, out):
    for ref, other, low in ((gate, other_gate, 0), (up, other_up, FF)):
        out[at[0], :, low : low + FF] = ref[...].astype(f32)
        out[1 - at[0], :, low : low + FF] = other[...].astype(f32)


def unshuffle_part(terms, order, me):
    half, unit = terms[0].shape[2:]
    (got,) = yield [(CORE, terms[1])]
    total = add(terms[0], got)
    (got,) = yield [("y", total[1].astype(bf16))]
    total = add(total[0], got).astype(bf16)
    blocks, marks = yield from exchange_blocks(total, order)
    mine = whole_call(
        functools.partial(spread_kernel, unit),
        jax.ShapeDtypeStruct((half, FF), bf16),
        [(me ^ f) // 2 for f in marks],
        [blocks],
        scratch=[pltpu.VMEM(blocks.shape, bf16)],
    )
    (other,) = yield [("y", mine)]
    return mine, other


def widen_gate_up(parts, s):
    mine, others = zip(*parts)
    half = mine[0].shape[0]
    whole = whole_call(
        widen_kernel,
        jax.ShapeDtypeStruct((2, half, 2 * FF), f32),
        [s],
        list(mine) + list(others),
    )
    return whole.reshape(2 * half, 2 * FF)


def sum_down(terms, core):
    give = lax.dynamic_index_in_dim(terms, 1 - core, 0, keepdims=False)
    (got,) = yield [(CORE, give)]
    part = add(lax.dynamic_index_in_dim(terms, core, 0, keepdims=False), got).astype(bf16)
    half = part.shape[0] // 2
    (low,) = yield [("y", part[:half])]
    (high,) = yield [("y", part[half:])]
    return add(part, join(low, high))


def rope_tables(positions):
    steps_half = jnp.arange(HD // 2, dtype=f32)
    inverse = rope_base ** (-2.0 * steps_half / HD)
    angles = positions.astype(f32)[:, None] * inverse
    cosines, sines = jnp.cos(angles), jnp.sin(angles)
    return join(cosines, cosines, axis=1), join(-sines, sines, axis=1)


def turn(head, cosines, sines):
    return head * cosines + pltpu.roll(head, HD // 2, 1) * sines


def rms_scale(values):
    return lax.rsqrt(jnp.mean(values * values, axis=-1, keepdims=True) + norm_eps)


def norm_backward(grad_normed, values, gain):
    scale_rows = rms_scale(values)
    scaled = grad_normed * gain
    gain_part = jnp.sum(grad_normed * values * scale_rows, axis=0, keepdims=True)
    grad_values = scale_rows * scaled - values * scale_rows**3 * jnp.mean(
        scaled * values, axis=-1, keepdims=True
    )
    return grad_values, gain_part


def head_at(index):
    return slice(index * HD, (index + 1) * HD)


def masks(second, ids_col, ids_row, other_row):
    shape = (ids_col.shape[0], ids_row.shape[1])
    rows = lax.broadcasted_iota(jnp.int32, shape, 0)
    cols = lax.broadcasted_iota(jnp.int32, shape, 1)
    near = (ids_col[...] == ids_row[...]) & (rows >= cols)
    far = (ids_col[...] == other_row[...]) & (rows + shape[0] * second >= shape[0])
    return near, far


def project_kernel(at, inputs, gain, weight, bias, cosines, sines, normed, queries, kv):
    values = inputs[...].astype(f32)
    rows = (values * rms_scale(values) * gain[...]).astype(bf16)
    normed[...] = rows
    projected = dot(rows, weight[...]) + bias[...]
    cos, sin = cosines[...], sines[...]
    for head in range(HQ):
        queries[:, head_at(head)] = turn(projected[:, head_at(head)], cos, sin).astype(bf16)
    for head in range(KV):
        kv[:, head_at(head)] = turn(projected[:, head_at(HQ + head)], cos, sin).astype(bf16)
    kv[:, KW:] = projected[:, QW + KW :].astype(bf16)


def attend_kernel(
    at, inputs, queries, kv, other, ids_col, ids_row, other_row, weight, gain,
    attended, logs, middle, normed,
):
    near, far = masks(at[0], ids_col, ids_row, other_row)
    factor = HD ** (-0.5)
    lanes = lax.broadcasted_iota(jnp.int32, logs.shape, 1)
    kept = jnp.zeros(logs.shape, f32)
    for head in range(HQ):
        k, v = head_at(head // GROUP), head_at(KV + head // GROUP)
        q = queries[:, head_at(head)]
        first = jnp.where(near, dot_t(q, kv[:, k]) * factor, -1e30)
        second = jnp.where(far, dot_t(q, other[:, k]) * factor, -1e30)
        peak = jnp.maximum(
            jnp.max(first, axis=-1, keepdims=True), jnp.max(second, axis=-1, keepdims=True)
        )
        total = jnp.sum(jnp.exp(first - peak), axis=-1, keepdims=True)
        total = total + jnp.sum(jnp.exp(second - peak), axis=-1, keepdims=True)
        log_total = peak + jnp.log(total)
        kept = jnp.where(lanes == head, log_total, kept)
        out = dot(jnp.exp(first - log_total).astype(bf16), kv[:, v])
        out = out + dot(jnp.exp(second - log_total).astype(bf16), other[:, v])
        attended[:, head_at(head)] = out.astype(bf16)
    logs[...] = kept
    rows = inputs[...].astype(f32) + dot(attended[...], weight[...])
    middle[...] = rows
    normed[...] = (rows * rms_scale(rows) * gain[...]).astype(bf16)


def attend_back_kernel(
    at, grad_normed, middle, gain, cotangent, weight, queries, kv, other,
    ids_col, ids_row, other_row, logs, cosines, sines,
    grad_middle, grad_branch, gain_part, grad_queries, keep, give,
):
    grad_values, part = norm_backward(grad_normed[...], middle[...], gain[...])
    gain_part[...] = part
    grad_rows = cotangent[...].astype(f32) + grad_values
    grad_middle[...] = grad_rows
    branch = grad_rows.astype(bf16)
    grad_branch[...] = branch
    grad_out = dot_t(branch, weight[...]).astype(bf16)
    near, far = masks(at[0], ids_col, ids_row, other_row)
    factor = HD ** (-0.5)
    lanes = lax.broadcasted_iota(jnp.int32, logs.shape, 1)
    cos, sin = cosines[...], -sines[...]
    for group in range(KV):
        k, v = head_at(group), head_at(KV + group)
        sums = [jnp.zeros((kv.shape[0], HD), f32) for _ in range(4)]
        for head in range(group * GROUP, (group + 1) * GROUP):
            q, g = queries[:, head_at(head)], grad_out[:, head_at(head)]
            log_total = jnp.sum(
                jnp.where(lanes == head, logs[...], 0.0), axis=-1, keepdims=True
            )
            first = jnp.where(near, dot_t(q, kv[:, k]) * factor, -1e30)
            second = jnp.where(far, dot_t(q, other[:, k]) * factor, -1e30)
            first, second = jnp.exp(first - log_total), jnp.exp(second - log_total)
            grad_first, grad_second = dot_t(g, kv[:, v]), dot_t(g, other[:, v])
            balance = jnp.sum(first * grad_first, axis=-1, keepdims=True)
            balance = balance + jnp.sum(second * grad_second, axis=-1, keepdims=True)
            grad_first = (first * (grad_first - balance)).astype(bf16)
            grad_second = (second * (grad_second - balance)).astype(bf16)
            grad_q = (dot(grad_first, kv[:, k]) + dot(grad_second, other[:, k])) * factor
            grad_q = turn(grad_q.astype(bf16).astype(f32), cos, sin)
            grad_queries[:, head_at(head)] = grad_q.astype(bf16)
            sums[0] = sums[0] + t_dot(grad_first, q)
            sums[1] = sums[1] + t_dot(first.astype(bf16), g)
            sums[2] = sums[2] + t_dot(grad_second, q)
            sums[3] = sums[3] + t_dot(second.astype(bf16), g)
        keep[:, k] = sums[0] * factor
        keep[:, v] = sums[1]
        give[:, k] = (sums[2] * factor).astype(bf16)
        give[:, v] = sums[3].astype(bf16)


def project_back_kernel(
    at, grad_queries, keep, got, cosines, sines, weight, inputs, gain, grad_middle,
    grad_projected, input_grad, gain_part, bias_part,
):
    grad_kv = (keep[...] + got[...].astype(f32)).astype(bf16)
    cos, sin = cosines[...], -sines[...]
    grad_projected[:, :QW] = grad_queries[...]
    for head in range(KV):
        grad_k = turn(grad_kv[:, head_at(head)].astype(f32), cos, sin)
        grad_projected[:, head_at(HQ + head)] = grad_k.astype(bf16)
    grad_projected[:, QW + KW :] = grad_kv[:, KW:]
    rows = grad_projected[...]
    bias_part[...] = jnp.sum(rows.astype(f32), axis=0, keepdims=True)
    grad_normed = dot_t(rows, weight[...])
    grad_values, part = norm_backward(grad_normed, inputs[...].astype(f32), gain[...])
    gain_part[...] = part
    input_grad[...] = grad_middle[...] + grad_values


def feed_kernel(
    tokens_a, tokens_b, cot_a, cot_b, gate_weight, up_weight, down_weight,
    hidden, grad_gate, grad_up, tokens, cotangent, back_a, back_b, total,
):
    step, steps = pl.program_id(0), pl.num_programs(0)
    half = tokens_a.shape[0]

    @pl.when(step == 0)
    def _():
        tokens[:half], tokens[half:] = tokens_a[...], tokens_b[...]
        cotangent[:half], cotangent[half:] = cot_a[...], cot_b[...]
        total[...] = jnp.zeros_like(total)

    gate = dot(tokens[...], gate_weight[...])
    up = dot(tokens[...], up_weight[...])
    grad_hidden = dot_t(cotangent[...], down_weight[...])
    sigmoid = jax.nn.sigmoid(gate)
    silu = gate * sigmoid
    hidden[...] = (silu * up).astype(bf16)
    gate_rows = (grad_hidden * up * sigmoid * (1.0 + gate * (1.0 - sigmoid))).astype(bf16)
    up_rows = (grad_hidden * silu).astype(bf16)
    grad_gate[...] = gate_rows
    grad_up[...] = up_rows
    total[...] += dot_t(
        join(gate_rows, up_rows, axis=1), join(gate_weight[...], up_weight[...], axis=1)
    )

    @pl.when(step == steps - 1)
    def _():
        back_a[...] = total[:half].astype(back_a.dtype)
        back_b[...] = total[half:].astype(back_b.dtype)


def feed_forward(tokens, cotangent, gate_up_weight, down_weight, back_type):
    half = tokens[0].shape[0]
    if half > 256 and half % 256 == 0:
        parts = [
            feed_forward(
                [v[low : low + 256] for v in tokens],
                [v[low : low + 256] for v in cotangent],
                gate_up_weight,
                down_weight,
                back_type,
            )
            for low in range(0, half, 256)
        ]
        halves = [
            join(*[part[i][low : low + 256] for low in (0, 256) for part in parts])
            for i in range(5)
        ]
        return (*halves, *[join(*[part[i] for part in parts]) for i in (5, 6)])
    rows = 2 * half
    padded = down_weight.shape[0]
    tile = 384
    steps = padded // tile
    whole = pl.BlockSpec((rows, D), lambda j: (0, 0))
    piece = pl.BlockSpec((half, D), lambda j: (0, 0))
    part = pl.BlockSpec((rows, tile), lambda j: (0, j))
    units = jax.ShapeDtypeStruct((rows, padded), bf16)
    lines = jax.ShapeDtypeStruct((rows, D), bf16)
    back = jax.ShapeDtypeStruct((half, D), back_type)
    return pl.pallas_call(
        feed_kernel,
        grid=(steps,),
        out_shape=(units, units, units, lines, lines, back, back),
        in_specs=[piece] * 4
        + [
            pl.BlockSpec((D, tile), lambda j: (0, j)),
            pl.BlockSpec((D, tile), lambda j: (0, j + steps)),
            pl.BlockSpec((tile, D), lambda j: (j, 0)),
        ],
        out_specs=(part, part, part, whole, whole, piece, piece),
        scratch_shapes=[pltpu.VMEM((rows, D), f32)],
        compiler_params=pltpu.CompilerParams(vmem_limit_bytes=VMEM),
        cost_estimate=pl.CostEstimate(
            flops=10 * rows * D * padded,
            bytes_accessed=6 * D * padded + 8 * rows * D + 6 * rows * padded,
            transcendentals=rows * padded,
        ),
    )(*tokens, *cotangent, gate_up_weight, gate_up_weight, down_weight)


def pair_kernel(at, own, other, out):
    rows = own.shape[0]
    for core, first, second in ((0, own, other), (1, other, own)):

        @pl.when(at[0] == core)
        def _():
            out[:rows], out[rows : 2 * rows] = first[...], second[...]

    if out.shape[0] > 2 * rows:
        out[2 * rows :] = jnp.zeros((out.shape[0] - 2 * rows, out.shape[1]), out.dtype)


def body(
    inputs,
    positions,
    segments,
    gain_one,
    qkv_weight,
    qkv_bias,
    out_weight,
    gain_two,
    gate_up_weight,
    down_weight,
    cotangent,
):
    tokens = inputs.shape[0] * inputs.shape[1]
    size = lax.axis_size("fsdp")
    me = lax.axis_index("fsdp")
    s = lax.axis_index("seq")
    unit = 2 * FF // size
    padded = -(-unit // 384) * 384

    lanes = Lanes()
    far = far_bits()
    core = me % 2
    input_rows = inputs.reshape(tokens, D)
    grad_rows = cotangent.reshape(tokens, D)
    gate_blocks, up_blocks = split_gate_up(gate_up_weight, me, s)
    cot_blocks, token_blocks = [], []
    qkv = Move(gather_weight(qkv_weight, me, s))
    out = Move(gather_weight_plain(out_weight, me))
    gate = Move(shuffle_part(gate_blocks, [X] + far + [Z]))
    up = Move(shuffle_part(up_blocks, [X] + far + [Z]))
    cot = Move(gather_tokens(grad_rows, cot_blocks))
    down = Move(swap(CORE, down_weight))
    lanes.round(qkv, up)
    lanes.round(qkv, (out, 2), gate)
    lanes.round(qkv)
    lanes.round(qkv, out, (gate, 2))
    lanes.round(qkv, out)
    (qkv_full,) = lanes.drain(qkv)

    rows_bf16 = jax.ShapeDtypeStruct((tokens, D), bf16)
    rows_f32 = jax.ShapeDtypeStruct((tokens, D), f32)
    cosines, sines = rope_tables(positions.reshape(tokens))
    ids = segments.reshape(2, tokens)
    ids_row = lax.dynamic_index_in_dim(ids, s, 0)
    other_row = lax.dynamic_index_in_dim(ids, 1 - s, 0)
    ids_col = ids_row.reshape(tokens, 1)
    gain_one, gain_two = gain_one[None], gain_two[None]
    normed, queries, kv = whole_call(
        project_kernel,
        (rows_bf16, rows_bf16, jax.ShapeDtypeStruct((tokens, 2 * KW), bf16)),
        [s],
        [input_rows, gain_one, qkv_full, qkv_bias[None], cosines, sines],
        flops=2 * tokens * D * (QW + 2 * KW),
    )
    lanes.beside(kv)
    other = Move(swap("y", kv))
    lanes.round(other, out, (up, 2), gate)
    other_kv, out_full = lanes.drain(other, out)
    attended, logs, middle, normed_two = whole_call(
        attend_kernel,
        (rows_bf16, jax.ShapeDtypeStruct((tokens, HD), f32), rows_f32, rows_bf16),
        [s],
        [input_rows, queries, kv, other_kv, ids_col, ids_row, other_row, out_full, gain_two],
        flops=2 * tokens * D * (D + 8 * tokens),
    )

    lanes.beside(normed_two)
    token = Move(gather_tokens(normed_two, token_blocks))
    lanes.round(token, gate, up)
    lanes.round(token, (cot, 2), (up, 2), down)
    lanes.round(token, gate)
    lanes.round(cot, up)
    parts = lanes.drain(gate, up)
    gate_up_full = weave_gate_up(parts, me, s)
    (other_down,) = lanes.drain(down)
    down_full = whole_call(
        pair_kernel,
        jax.ShapeDtypeStruct((padded, D), bf16),
        [core],
        [down_weight, other_down],
    )
    lanes.drain(token, cot)
    early = feed_forward(token_blocks[0], cot_blocks[0], gate_up_full, down_full, f32)
    last = feed_forward(
        [after(token_blocks[1][0], early[5]), token_blocks[1][1]],
        cot_blocks[1],
        gate_up_full,
        down_full,
        bf16,
    )
    back = Move(scatter_tokens(early[5:], last[5:]))
    lanes.round(back)

    half = last[5].shape[0]
    gate_terms = gate_up_grad([early[3], last[3]], [early[1], last[1]], me, s)
    out_terms = [[dot(v[0][:half], down_full), dot(v[0][half:], down_full)] for v in (early, last)]
    gate = Move(unshuffle_part(gate_terms, far + [Z, X], me))
    result = Move(scatter_tokens(out_terms[0], [term.astype(bf16) for term in out_terms[1]]))
    lanes.round(back, gate)
    up_terms = gate_up_grad(
        [early[3], last[3]], [lanes.hold(early[2]), lanes.hold(last[2])], me, s
    )
    up = Move(unshuffle_part(up_terms, [X, Z] + far, me))
    lanes.round(back, gate, result, up)
    down_terms = t_dot(lanes.hold(early[0]), early[4]) + t_dot(lanes.hold(last[0]), last[4])
    down_terms = down_terms[:unit].astype(bf16).reshape(2, unit // 2, D)
    down = Move(sum_down(down_terms, core))
    (grad_normed_two,) = lanes.drain(back)
    lanes.round(result, (gate, 2), (up, 2))

    grad_middle, grad_branch, gain_two_part, grad_queries, keep, give = whole_call(
        attend_back_kernel,
        (
            rows_f32,
            rows_bf16,
            jax.ShapeDtypeStruct((1, D), f32),
            rows_bf16,
            jax.ShapeDtypeStruct((tokens, 2 * KW), f32),
            jax.ShapeDtypeStruct((tokens, 2 * KW), bf16),
        ),
        [s],
        [grad_normed_two, middle, gain_two, grad_rows, out_full, queries, kv, other_kv]
        + [ids_col, ids_row, other_row, logs, cosines, sines],
        flops=2 * tokens * D * (D + 20 * tokens),
    )
    other = Move(swap("y", give))
    lanes.more(other)
    (got,) = lanes.drain(other)
    out = Move(scatter_weight(attended, grad_branch, me, s))
    grad_projected, input_grad, gain_one_part, bias_part = whole_call(
        project_back_kernel,
        (
            jax.ShapeDtypeStruct((tokens, QW + 2 * KW), bf16),
            rows_f32,
            jax.ShapeDtypeStruct((1, D), f32),
            jax.ShapeDtypeStruct((1, QW + 2 * KW), f32),
        ),
        [s],
        [grad_queries, keep, got, cosines, sines, qkv_full, input_rows, gain_one, grad_middle],
        flops=2 * tokens * D * (QW + 2 * KW),
    )
    lanes.beside(grad_projected)
    qkv = Move(scatter_weight(normed, grad_projected, me, s))
    sums = Move(sum_everywhere(join(gain_one_part[0], bias_part[0], gain_two_part[0])))
    lanes.round(qkv, down)
    lanes.round(qkv, (result, 2), out, down)
    lanes.round(qkv, gate, up, sums)
    lanes.round(qkv, gate, up, down, sums)
    lanes.round(qkv, out, (up, 2), (gate, 2), sums)
    lanes.round(qkv, out, sums)
    lanes.round(out, up, sums)
    qkv_weight_total, out_weight_total, down_total, out_sum, sums, *parts = lanes.drain(
        qkv, out, down, result, sums, gate, up
    )
    gate_up_total = widen_gate_up(parts, s)
    output = (middle + out_sum).astype(bf16).reshape(inputs.shape)
    width = bias_part.shape[1]
    return (
        output,
        input_grad.reshape(inputs.shape),
        sums[:D],
        qkv_weight_total,
        sums[D : D + width],
        out_weight_total,
        sums[D + width :],
        gate_up_total,
        down_total,
    )


def solution(mesh):
    placed = (
        P("fsdp", "seq", None),
        P("fsdp", "seq"),
        P("fsdp", None),
        P(),
        P("fsdp", None),
        P(),
        P("fsdp", None),
        P(),
        P("fsdp", None),
        P("fsdp", None),
        P("fsdp", "seq", None),
    )
    return jax.shard_map(
        body,
        mesh=mesh,
        in_specs=placed,
        out_specs=(
            P("fsdp", "seq", None),
            P("fsdp", "seq", None),
            P(),
            P("fsdp", None),
            P(),
            P("fsdp", None),
            P(),
            P("fsdp", None),
            P("fsdp", None),
        ),
        check_vma=False,
    )
```

```python
import functools

import jax
import jax.numpy as jnp
from jax import lax
from jax.experimental import pallas as pl
from jax.experimental.pallas import tpu as pltpu
from jax.sharding import PartitionSpec as P

D = 1536
FF = 8960
HQ = 12
KV = 2
HD = 128
GROUP = HQ // KV
QW = HQ * HD
KW = KV * HD

rope_base = 1000000.0
norm_eps = 1e-06
bf16 = jnp.bfloat16
f32 = jnp.float32


CORE, X, Z = 1, 2, 4
ROTATED = ((Z, X, "y"), (X, "y", Z), ("y", Z, X))
CROSSED = ((X, Z), (Z, X))
VMEM = 48 * 1024 * 1024


def far_bits():
    return [bit for bit in (8 << i for i in range(16)) if bit < lax.axis_size("fsdp")]


def after(value, *earlier):
    return lax.optimization_barrier((value,) + earlier)[0]


class Move:
    def __init__(self, steps):
        self.steps = steps
        self.result = self.arrived = None
        self.wanted = next(steps)

    def resume(self, beside=()):
        if self.arrived is None:
            return
        arrived, self.arrived = self.arrived, None
        if beside:
            arrived = [after(value, *beside) for value in arrived]
        try:
            self.wanted = self.steps.send(arrived)
        except StopIteration as stop:
            self.result = stop.value


class Lanes:
    def __init__(self):
        self.flying, self.ended, self.before, self.kernels = [], [], [], []

    def round(self, *entries):
        ended = [value for value, left in self.flying if left <= 1] + self.kernels
        self.before, self.ended = ended + self.ended, ended
        self.flying = [(value, left - 1) for value, left in self.flying if left > 1]
        self.waited, self.kernels = self.kernels, []
        self.more(*entries)

    def more(self, *entries):
        size = lax.axis_size("fsdp")
        for entry in entries:
            move, lasts = entry if isinstance(entry, tuple) else (entry, 1)
            move.resume(self.waited)
            if not move.wanted:
                continue
            move.arrived = []
            for link, value in move.wanted:
                if self.before:
                    value = after(value, *self.before)
                if link == "y":
                    value = lax.ppermute(value, "seq", [(0, 1), (1, 0)])
                else:
                    value = lax.ppermute(value, "fsdp", [(i, i ^ link) for i in range(size)])
                move.arrived.append(value)
                self.flying.append((value, lasts))
            move.wanted = None

    def hold(self, value):
        return after(value, *self.before) if self.before else value

    def beside(self, *values):
        self.kernels += values

    def drain(self, *moves):
        for move in moves:
            move.resume()
        while any(move.wanted for move in moves):
            self.round(*moves)
            for move in moves:
                move.resume()
        return [move.result for move in moves]


def add(left, right):
    return left.astype(f32) + right.astype(f32)


def dot(left, right):
    return jnp.dot(left, right, preferred_element_type=f32)


def dot_t(left, right):
    return lax.dot_general(left, right, (((1,), (1,)), ((), ())), preferred_element_type=f32)


def t_dot(left, right):
    return lax.dot_general(left, right, (((0,), (0,)), ((), ())), preferred_element_type=f32)


def join(*pieces, axis=0):
    return jnp.concatenate(pieces, axis=axis)


def pick(value, index, axis):
    return lax.index_in_dim(value, index, axis, keepdims=False)


def whole_call(kernel, out_shape, scalars, arrays, scratch=(), flops=0):
    outs = out_shape if isinstance(out_shape, (list, tuple)) else [out_shape]
    moved = sum(a.size * a.dtype.itemsize for a in list(arrays) + list(outs))
    spec = pl.BlockSpec(memory_space=pltpu.VMEM)
    return pl.pallas_call(
        kernel,
        out_shape=out_shape,
        in_specs=[pl.BlockSpec(memory_space=pltpu.SMEM)] + [spec] * len(arrays),
        out_specs=jax.tree.map(lambda _: spec, out_shape),
        scratch_shapes=list(scratch),
        compiler_params=pltpu.CompilerParams(vmem_limit_bytes=VMEM),
        cost_estimate=pl.CostEstimate(flops=flops, bytes_accessed=moved, transcendentals=0),
    )(jnp.stack(scalars).astype(jnp.int32), *arrays)


def gather_tokens(rows, blocks):
    state = rows[None]
    for bit in far_bits():
        (got,) = yield [(bit, state)]
        state = join(state, got)
    half, width = rows.shape[0] // 2, rows.shape[1]
    first, second = state[:, :half], state[:, half:]
    got = yield [(Z, first), (X, second)]
    first, second = join(first, got[0]), join(second, got[1])
    blocks.append([v.reshape(-1, width) for v in (first, second)])
    last = yield [(X, first), (Z, second)]
    blocks.append([v.reshape(-1, width) for v in last])


def scatter_tokens(early, last):
    width = last[0].shape[1]
    far = far_bits()
    count = 1 << len(far)
    half = last[0].shape[0] // count // 2
    got = yield [(X, last[0]), (Z, last[1])]
    first = add(early[0], got[0]).reshape(2, count, half, width)
    second = add(early[1], got[1]).reshape(2, count, half, width)
    got = yield [(Z, first[1].astype(bf16)), (X, second[1].astype(bf16))]
    state = join(add(first[0], got[0]), add(second[0], got[1]), axis=1)
    for bit in reversed(far):
        count //= 2
        (got,) = yield [(bit, state[count:].astype(bf16))]
        state = add(state[:count], got)
    return state[0]


def place_kernel(where, *refs):
    out = refs[-1]
    at = 0
    for ref in refs[:-1]:
        for i in range(ref.shape[0]):
            out[where[at]] = ref[i]
            at += 1


def cut_columns(width):
    third = width // 3 // 128 * 128
    return ((0, third), (third, 2 * third), (2 * third, width))


def gather_weight(shard, me, s):
    size = lax.axis_size("fsdp")
    half, width = shard.shape[0] // 2, shard.shape[1]
    state = lax.dynamic_index_in_dim(shard.reshape(2, half, width), s, 0)
    marks = [(0, 0)]
    for bit in far_bits():
        (got,) = yield [(bit, state)]
        state = join(state, got)
        marks = marks + [(f ^ bit, h) for f, h in marks]
    states = [state[:, :, low:high] for low, high in cut_columns(width)]
    for step in range(3):
        got = yield [(ROTATED[part][step], states[part]) for part in range(3)]
        states = [join(*pair) for pair in zip(states, got)]
    turns = []
    for order in ROTATED:
        index = [order.index(link) for link in reversed(ROTATED[0])]
        turns.append([2 - i for i in index])
    count = len(marks)
    split = [v.reshape(2, 2, 2, count, half, v.shape[-1]) for v in states]
    state = join(*[jnp.transpose(v, t + [3, 4, 5]) for v, t in zip(split, turns)], axis=-1)
    state = state.reshape(8 * count, half, width)
    for link in ROTATED[0]:
        marks = marks + [(f, 1 - h) if link == "y" else (f ^ link, h) for f, h in marks]
    (got,) = yield [(CORE, state)]
    where = []
    for core in range(2):
        where += [(me ^ f ^ core) * 2 + (s ^ h) for f, h in marks]
    whole = whole_call(
        place_kernel,
        jax.ShapeDtypeStruct((size * 2, half, width), bf16),
        where,
        [state, got],
    )
    return whole.reshape(size * 2 * half, width)


def gather_weight_plain(shard, me):
    size = lax.axis_size("fsdp")
    rows, width = shard.shape
    state = shard[None]
    marks = [0]
    for bit in far_bits():
        (got,) = yield [(bit, state)]
        state = join(state, got)
        marks = marks + [f ^ bit for f in marks]
    cut = width // 3 // 128 * 128
    first, second = state[:, :, :cut], state[:, :, cut:]
    got = yield [(X, first), (Z, second)]
    first, second = join(first, got[0]), join(second, got[1])
    got = yield [(Z, first), (X, second)]
    count = len(marks)
    second = join(second[:count], got[1][:count], second[count:], got[1][count:])
    state = join(join(first, got[0]), second, axis=2)
    for link in (X, Z):
        marks = marks + [f ^ link for f in marks]
    (got,) = yield [(CORE, state)]
    where = [me ^ f for f in marks] + [me ^ f ^ CORE for f in marks]
    whole = whole_call(
        place_kernel, jax.ShapeDtypeStruct((size, rows, width), bf16), where, [state, got]
    )
    return whole.reshape(size * rows, width)


def order_kernel(where, source, out):
    for i in range(source.shape[0]):
        out[where[i]] = source[i]


def turn_rows(left, me, s):
    size = lax.axis_size("fsdp")
    count = size // 8
    rows = left.shape[1]
    turned = left.T.reshape(size * 2, rows // size // 2, left.shape[0])
    where = []
    for place in range(size):
        for h in range(2):
            k = me ^ place
            kept = ((k % 2) * 2 + (k // 2) % 2) * 2 + (k // 4) % 2
            where.append((kept * count + k // 8) * 2 + (s ^ h))
    return whole_call(
        order_kernel, jax.ShapeDtypeStruct(turned.shape, bf16), where, [turned]
    ).reshape(2, rows // 2, left.shape[0])


def scatter_weight(turned, right, s, cut):
    size = lax.axis_size("fsdp")
    far = far_bits()
    count = 1 << len(far)
    half, width = turned.shape[1] // size, right.shape[1]
    (got,) = yield [(CORE, dot(turned[1], right).astype(bf16))]
    total = add(dot(turned[0], right), got).reshape(2, 2, count, 2, half, width)
    low, high = total[..., :cut], total[..., cut:]
    got = yield [(X, low[1].astype(bf16)), (Z, high[:, 1].astype(bf16))]
    low, high = add(low[0], got[0]), add(high[:, 0], got[1])
    got = yield [(Z, low[1].astype(bf16)), (X, high[1].astype(bf16))]
    state = join(add(low[0], got[0]), add(high[0], got[1]), axis=-1)
    for bit in reversed(far):
        count //= 2
        (got,) = yield [(bit, state[count:].astype(bf16))]
        state = add(state[:count], got)
    (got,) = yield [("y", state[0, 1].astype(bf16))]
    mine = add(state[0, 0], got).astype(bf16)
    (other,) = yield [("y", mine)]
    low = jnp.where(s == 0, mine, other)
    high = jnp.where(s == 0, other, mine)
    return join(low, high).astype(f32)


def sum_everywhere(value):
    for link in [CORE, X, Z] + far_bits() + ["y"]:
        (got,) = yield [(link, value)]
        value = value + got
    return value


def swap(link, value):
    (got,) = yield [(link, value)]
    return got


def exchange_blocks(blocks, order):
    axes = list(reversed(far_bits())) + [Z, X]
    state = blocks.reshape((1,) + (2,) * len(axes) + blocks.shape[1:])
    marks = [0]
    for link in order:
        axis = 1 + axes.index(link)
        axes.remove(link)
        (got,) = yield [(link, pick(state, 1, axis))]
        state = join(pick(state, 0, axis), got)
        marks = marks + [f ^ link for f in marks]
    return state, marks


def split_kernel(unit, at, shard, gate, up):
    for chip in range(gate.shape[0]):
        low = chip * unit
        gate[at[0] ^ chip] = shard[at[1], :, low : low + unit]
        up[at[0] ^ chip] = shard[at[1], :, FF + low : FF + low + unit]


def weave_kernel(unit, where, *refs):
    out = refs[-1]
    half, padded = out.shape[1], out.shape[2] // 2
    at = 0
    for part in range(2):
        low = part * padded
        for ref in refs[3 * part : 3 * part + 3]:
            for i in range(ref.shape[0]):
                out[where[at], :, low : low + unit] = ref[i]
                if padded > unit:
                    out[where[at], :, low + unit : low + padded] = jnp.zeros(
                        (half, padded - unit), out.dtype
                    )
                at += 1


def split_gate_up(shard, me, s):
    size = lax.axis_size("fsdp")
    half = shard.shape[0] // 2
    unit = 2 * FF // size
    block = jax.ShapeDtypeStruct((size // 2, half, unit), bf16)
    return whole_call(
        functools.partial(split_kernel, unit),
        (block, block),
        [me // 2, s],
        [shard.reshape(2, half, 2 * FF)],
    )


def shuffle_part(blocks, order):
    mine, marks = yield from exchange_blocks(blocks, order)
    (other,) = yield [("y", mine)]
    (got,) = yield [(CORE, join(mine, other))]
    return [mine, other, got], marks


def weave_gate_up(parts, me, s):
    size = lax.axis_size("fsdp")
    half, unit = parts[0][0][0].shape[1:]
    padded = -(-unit // 384) * 384
    pieces, where = [], []
    for blocks, marks in parts:
        pieces += blocks
        for core in range(2):
            for h in range(2):
                where += [(me ^ f ^ core) * 2 + (s ^ h) for f in marks]
    whole = whole_call(
        functools.partial(weave_kernel, unit),
        jax.ShapeDtypeStruct((size * 2, half, 2 * padded), bf16),
        where,
        pieces,
    )
    return whole.reshape(size * 2 * half, 2 * padded)


def grad_kernel(count, unit, at, *refs):
    outs = refs[-2:]
    half = outs[0].shape[2]
    total = 0.0
    for j in range(count):
        total = total + t_dot(refs[j][...], refs[count + j][...])
    total = total.astype(bf16)[:, :unit]
    here = total.shape[0] // (2 * half)
    for i in range(here):
        k = at[0] ^ (pl.program_id(0) * here + i)
        for h in range(2):
            low = (2 * i + h) * half
            for core, out in enumerate(outs):

                @pl.when(k % 2 == core)
                def _():
                    out[at[1] ^ h, k // 2] = total[low : low + half]


def gate_up_grad(token_blocks, grad_blocks, me, s):
    size = lax.axis_size("fsdp")
    unit = 2 * FF // size
    padded = grad_blocks[0].shape[1]
    half = D // size // 2
    count = len(token_blocks)
    rows = token_blocks[0].shape[0]
    tile = 768
    return pl.pallas_call(
        functools.partial(grad_kernel, count, unit),
        out_shape=[jax.ShapeDtypeStruct((2, size // 2, half, unit), bf16)] * 2,
        grid=(D // tile,),
        in_specs=[pl.BlockSpec(memory_space=pltpu.SMEM)]
        + [pl.BlockSpec((rows, tile), lambda i: (0, i))] * count
        + [pl.BlockSpec((rows, padded), lambda i: (0, 0))] * count,
        out_specs=[pl.BlockSpec(memory_space=pltpu.VMEM)] * 2,
        compiler_params=pltpu.CompilerParams(vmem_limit_bytes=VMEM),
        cost_estimate=pl.CostEstimate(
            flops=2 * count * rows * D * padded,
            bytes_accessed=2 * count * rows * (D + padded) + 4 * D * unit,
            transcendentals=0,
        ),
    )(jnp.stack([me, s]).astype(jnp.int32), *token_blocks, *grad_blocks)


def spread_kernel(unit, where, blocks, out, held):
    for i in range(blocks.shape[0]):
        held[where[i]] = blocks[i]
    for chip in range(blocks.shape[0]):
        out[:, chip * unit : (chip + 1) * unit] = held[chip]


def widen_kernel(at, gate, up, other_gate, other_up, out):
    for ref, other, low in ((gate, other_gate, 0), (up, other_up, FF)):
        out[at[0], :, low : low + FF] = ref[...].astype(f32)
        out[1 - at[0], :, low : low + FF] = other[...].astype(f32)


def unshuffle_part(terms, order, me):
    half, unit = terms[0].shape[2:]
    (got,) = yield [(CORE, terms[1])]
    total = add(terms[0], got)
    (got,) = yield [("y", total[1].astype(bf16))]
    total = add(total[0], got).astype(bf16)
    blocks, marks = yield from exchange_blocks(total, order)
    mine = whole_call(
        functools.partial(spread_kernel, unit),
        jax.ShapeDtypeStruct((half, FF), bf16),
        [(me ^ f) // 2 for f in marks],
        [blocks],
        scratch=[pltpu.VMEM(blocks.shape, bf16)],
    )
    (other,) = yield [("y", mine)]
    return mine, other


def widen_gate_up(parts, s):
    mine, others = zip(*parts)
    half = mine[0].shape[0]
    whole = whole_call(
        widen_kernel,
        jax.ShapeDtypeStruct((2, half, 2 * FF), f32),
        [s],
        list(mine) + list(others),
    )
    return whole.reshape(2 * half, 2 * FF)


def sum_down(terms, core):
    give = lax.dynamic_index_in_dim(terms, 1 - core, 0, keepdims=False)
    (got,) = yield [(CORE, give)]
    part = add(lax.dynamic_index_in_dim(terms, core, 0, keepdims=False), got).astype(bf16)
    half = part.shape[0] // 2
    (low,) = yield [("y", part[:half])]
    (high,) = yield [("y", part[half:])]
    return add(part, join(low, high))


def rope_tables(positions):
    steps_half = jnp.arange(HD // 2, dtype=f32)
    inverse = rope_base ** (-2.0 * steps_half / HD)
    angles = positions.astype(f32)[:, None] * inverse
    cosines, sines = jnp.cos(angles), jnp.sin(angles)
    return join(cosines, cosines, axis=1), join(-sines, sines, axis=1)


def turn(head, cosines, sines):
    return head * cosines + pltpu.roll(head, HD // 2, 1) * sines


def rms_scale(values):
    return lax.rsqrt(jnp.mean(values * values, axis=-1, keepdims=True) + norm_eps)


def norm_backward(grad_normed, values, gain):
    scale_rows = rms_scale(values)
    scaled = grad_normed * gain
    gain_part = jnp.sum(grad_normed * values * scale_rows, axis=0, keepdims=True)
    grad_values = scale_rows * scaled - values * scale_rows**3 * jnp.mean(
        scaled * values, axis=-1, keepdims=True
    )
    return grad_values, gain_part


def head_at(index):
    return slice(index * HD, (index + 1) * HD)


def masks(second, ids_col, ids_row, other_row):
    shape = (ids_col.shape[0], ids_row.shape[1])
    rows = lax.broadcasted_iota(jnp.int32, shape, 0)
    cols = lax.broadcasted_iota(jnp.int32, shape, 1)
    near = (ids_col[...] == ids_row[...]) & (rows >= cols)
    far = (ids_col[...] == other_row[...]) & (rows + shape[0] * second >= shape[0])
    return near, far


def project_kernel(at, inputs, gain, weight, bias, cosines, sines, normed, queries, kv):
    values = inputs[...].astype(f32)
    rows = (values * rms_scale(values) * gain[...]).astype(bf16)
    normed[...] = rows
    projected = dot(rows, weight[...]) + bias[...]
    cos, sin = cosines[...], sines[...]
    for head in range(HQ):
        queries[:, head_at(head)] = turn(projected[:, head_at(head)], cos, sin).astype(bf16)
    for head in range(KV):
        kv[:, head_at(head)] = turn(projected[:, head_at(HQ + head)], cos, sin).astype(bf16)
    kv[:, KW:] = projected[:, QW + KW :].astype(bf16)


def attend_kernel(
    at, inputs, queries, kv, other, ids_col, ids_row, other_row, weight, gain,
    attended, logs, middle, normed,
):
    near, far = masks(at[0], ids_col, ids_row, other_row)
    factor = HD ** (-0.5)
    lanes = lax.broadcasted_iota(jnp.int32, logs.shape, 1)
    kept = jnp.zeros(logs.shape, f32)
    for head in range(HQ):
        k, v = head_at(head // GROUP), head_at(KV + head // GROUP)
        q = queries[:, head_at(head)]
        first = jnp.where(near, dot_t(q, kv[:, k]) * factor, -1e30)
        second = jnp.where(far, dot_t(q, other[:, k]) * factor, -1e30)
        peak = jnp.maximum(
            jnp.max(first, axis=-1, keepdims=True), jnp.max(second, axis=-1, keepdims=True)
        )
        total = jnp.sum(jnp.exp(first - peak), axis=-1, keepdims=True)
        total = total + jnp.sum(jnp.exp(second - peak), axis=-1, keepdims=True)
        log_total = peak + jnp.log(total)
        kept = jnp.where(lanes == head, log_total, kept)
        out = dot(jnp.exp(first - log_total).astype(bf16), kv[:, v])
        out = out + dot(jnp.exp(second - log_total).astype(bf16), other[:, v])
        attended[:, head_at(head)] = out.astype(bf16)
    logs[...] = kept
    rows = inputs[...].astype(f32) + dot(attended[...], weight[...])
    middle[...] = rows
    normed[...] = (rows * rms_scale(rows) * gain[...]).astype(bf16)


def attend_back_kernel(
    at, grad_normed, middle, gain, cotangent, weight, queries, kv, other,
    ids_col, ids_row, other_row, logs, cosines, sines,
    grad_middle, grad_branch, gain_part, grad_queries, keep, give,
):
    grad_values, part = norm_backward(grad_normed[...], middle[...], gain[...])
    gain_part[...] = part
    grad_rows = cotangent[...].astype(f32) + grad_values
    grad_middle[...] = grad_rows
    branch = grad_rows.astype(bf16)
    grad_branch[...] = branch
    grad_out = dot_t(branch, weight[...]).astype(bf16)
    near, far = masks(at[0], ids_col, ids_row, other_row)
    factor = HD ** (-0.5)
    lanes = lax.broadcasted_iota(jnp.int32, logs.shape, 1)
    cos, sin = cosines[...], -sines[...]
    for group in range(KV):
        k, v = head_at(group), head_at(KV + group)
        sums = [jnp.zeros((kv.shape[0], HD), f32) for _ in range(4)]
        for head in range(group * GROUP, (group + 1) * GROUP):
            q, g = queries[:, head_at(head)], grad_out[:, head_at(head)]
            log_total = jnp.sum(
                jnp.where(lanes == head, logs[...], 0.0), axis=-1, keepdims=True
            )
            first = jnp.where(near, dot_t(q, kv[:, k]) * factor, -1e30)
            second = jnp.where(far, dot_t(q, other[:, k]) * factor, -1e30)
            first, second = jnp.exp(first - log_total), jnp.exp(second - log_total)
            grad_first, grad_second = dot_t(g, kv[:, v]), dot_t(g, other[:, v])
            balance = jnp.sum(first * grad_first, axis=-1, keepdims=True)
            balance = balance + jnp.sum(second * grad_second, axis=-1, keepdims=True)
            grad_first = (first * (grad_first - balance)).astype(bf16)
            grad_second = (second * (grad_second - balance)).astype(bf16)
            grad_q = (dot(grad_first, kv[:, k]) + dot(grad_second, other[:, k])) * factor
            grad_q = turn(grad_q.astype(bf16).astype(f32), cos, sin)
            grad_queries[:, head_at(head)] = grad_q.astype(bf16)
            sums[0] = sums[0] + t_dot(grad_first, q)
            sums[1] = sums[1] + t_dot(first.astype(bf16), g)
            sums[2] = sums[2] + t_dot(grad_second, q)
            sums[3] = sums[3] + t_dot(second.astype(bf16), g)
        keep[:, k] = sums[0] * factor
        keep[:, v] = sums[1]
        give[:, k] = (sums[2] * factor).astype(bf16)
        give[:, v] = sums[3].astype(bf16)


def project_back_kernel(
    at, grad_queries, keep, got, cosines, sines, weight, inputs, gain, grad_middle,
    grad_projected, input_grad, gain_part, bias_part,
):
    grad_kv = (keep[...] + got[...].astype(f32)).astype(bf16)
    cos, sin = cosines[...], -sines[...]
    grad_projected[:, :QW] = grad_queries[...]
    for head in range(KV):
        grad_k = turn(grad_kv[:, head_at(head)].astype(f32), cos, sin)
        grad_projected[:, head_at(HQ + head)] = grad_k.astype(bf16)
    grad_projected[:, QW + KW :] = grad_kv[:, KW:]
    rows = grad_projected[...]
    bias_part[...] = jnp.sum(rows.astype(f32), axis=0, keepdims=True)
    grad_normed = dot_t(rows, weight[...])
    grad_values, part = norm_backward(grad_normed, inputs[...].astype(f32), gain[...])
    gain_part[...] = part
    input_grad[...] = grad_middle[...] + grad_values


def feed_kernel(
    tokens_a, tokens_b, cot_a, cot_b, gate_weight, up_weight, down_weight,
    hidden, grad_gate, grad_up, tokens, cotangent, back_a, back_b, total,
):
    step, steps = pl.program_id(0), pl.num_programs(0)
    half = tokens_a.shape[0]

    @pl.when(step == 0)
    def _():
        tokens[:half], tokens[half:] = tokens_a[...], tokens_b[...]
        cotangent[:half], cotangent[half:] = cot_a[...], cot_b[...]
        total[...] = jnp.zeros_like(total)

    gate = dot(tokens[...], gate_weight[...])
    up = dot(tokens[...], up_weight[...])
    grad_hidden = dot_t(cotangent[...], down_weight[...])
    sigmoid = jax.nn.sigmoid(gate)
    silu = gate * sigmoid
    hidden[...] = (silu * up).astype(bf16)
    gate_rows = (grad_hidden * up * sigmoid * (1.0 + gate * (1.0 - sigmoid))).astype(bf16)
    up_rows = (grad_hidden * silu).astype(bf16)
    grad_gate[...] = gate_rows
    grad_up[...] = up_rows
    total[...] += dot_t(
        join(gate_rows, up_rows, axis=1), join(gate_weight[...], up_weight[...], axis=1)
    )

    @pl.when(step == steps - 1)
    def _():
        back_a[...] = total[:half].astype(back_a.dtype)
        back_b[...] = total[half:].astype(back_b.dtype)


def feed_forward(tokens, cotangent, gate_up_weight, down_weight, back_type):
    half = tokens[0].shape[0]
    if half > 256 and half % 256 == 0:
        parts = [
            feed_forward(
                [v[low : low + 256] for v in tokens],
                [v[low : low + 256] for v in cotangent],
                gate_up_weight,
                down_weight,
                back_type,
            )
            for low in range(0, half, 256)
        ]
        halves = [
            join(*[part[i][low : low + 256] for low in (0, 256) for part in parts])
            for i in range(5)
        ]
        return (*halves, *[join(*[part[i] for part in parts]) for i in (5, 6)])
    rows = 2 * half
    padded = down_weight.shape[0]
    tile = 384
    steps = padded // tile
    whole = pl.BlockSpec((rows, D), lambda j: (0, 0))
    piece = pl.BlockSpec((half, D), lambda j: (0, 0))
    part = pl.BlockSpec((rows, tile), lambda j: (0, j))
    units = jax.ShapeDtypeStruct((rows, padded), bf16)
    lines = jax.ShapeDtypeStruct((rows, D), bf16)
    back = jax.ShapeDtypeStruct((half, D), back_type)
    return pl.pallas_call(
        feed_kernel,
        grid=(steps,),
        out_shape=(units, units, units, lines, lines, back, back),
        in_specs=[piece] * 4
        + [
            pl.BlockSpec((D, tile), lambda j: (0, j)),
            pl.BlockSpec((D, tile), lambda j: (0, j + steps)),
            pl.BlockSpec((tile, D), lambda j: (j, 0)),
        ],
        out_specs=(part, part, part, whole, whole, piece, piece),
        scratch_shapes=[pltpu.VMEM((rows, D), f32)],
        compiler_params=pltpu.CompilerParams(vmem_limit_bytes=VMEM),
        cost_estimate=pl.CostEstimate(
            flops=10 * rows * D * padded,
            bytes_accessed=6 * D * padded + 8 * rows * D + 6 * rows * padded,
            transcendentals=rows * padded,
        ),
    )(*tokens, *cotangent, gate_up_weight, gate_up_weight, down_weight)


def pair_kernel(at, own, other, out):
    rows = own.shape[0]
    for core, first, second in ((0, own, other), (1, other, own)):

        @pl.when(at[0] == core)
        def _():
            out[:rows], out[rows : 2 * rows] = first[...], second[...]

    if out.shape[0] > 2 * rows:
        out[2 * rows :] = jnp.zeros((out.shape[0] - 2 * rows, out.shape[1]), out.dtype)


def body(
    inputs,
    positions,
    segments,
    gain_one,
    qkv_weight,
    qkv_bias,
    out_weight,
    gain_two,
    gate_up_weight,
    down_weight,
    cotangent,
):
    tokens = inputs.shape[0] * inputs.shape[1]
    size = lax.axis_size("fsdp")
    me = lax.axis_index("fsdp")
    s = lax.axis_index("seq")
    unit = 2 * FF // size
    padded = -(-unit // 384) * 384

    lanes = Lanes()
    far = far_bits()
    core = me % 2
    input_rows = inputs.reshape(tokens, D)
    grad_rows = cotangent.reshape(tokens, D)
    gate_blocks, up_blocks = split_gate_up(gate_up_weight, me, s)
    cot_blocks, token_blocks = [], []
    qkv = Move(gather_weight(qkv_weight, me, s))
    out = Move(gather_weight_plain(out_weight, me))
    gate = Move(shuffle_part(gate_blocks, [X] + far + [Z]))
    up = Move(shuffle_part(up_blocks, [X] + far + [Z]))
    cot = Move(gather_tokens(grad_rows, cot_blocks))
    down = Move(swap(CORE, down_weight))
    lanes.round(qkv, up)
    lanes.round(qkv, (out, 2), gate)
    lanes.round(qkv)
    lanes.round(qkv, out, (gate, 2))
    lanes.round(qkv, out)
    (qkv_full,) = lanes.drain(qkv)

    rows_bf16 = jax.ShapeDtypeStruct((tokens, D), bf16)
    rows_f32 = jax.ShapeDtypeStruct((tokens, D), f32)
    cosines, sines = rope_tables(positions.reshape(tokens))
    ids = segments.reshape(2, tokens)
    ids_row = lax.dynamic_index_in_dim(ids, s, 0)
    other_row = lax.dynamic_index_in_dim(ids, 1 - s, 0)
    ids_col = ids_row.reshape(tokens, 1)
    gain_one, gain_two = gain_one[None], gain_two[None]
    normed, queries, kv = whole_call(
        project_kernel,
        (rows_bf16, rows_bf16, jax.ShapeDtypeStruct((tokens, 2 * KW), bf16)),
        [s],
        [input_rows, gain_one, qkv_full, qkv_bias[None], cosines, sines],
        flops=2 * tokens * D * (QW + 2 * KW),
    )
    lanes.beside(kv)
    other = Move(swap("y", kv))
    lanes.round(other, out, (up, 2), gate)
    other_kv, out_full = lanes.drain(other, out)
    attended, logs, middle, normed_two = whole_call(
        attend_kernel,
        (rows_bf16, jax.ShapeDtypeStruct((tokens, HD), f32), rows_f32, rows_bf16),
        [s],
        [input_rows, queries, kv, other_kv, ids_col, ids_row, other_row, out_full, gain_two],
        flops=2 * tokens * D * (D + 8 * tokens),
    )

    lanes.beside(normed_two)
    token = Move(gather_tokens(normed_two, token_blocks))
    lanes.round(token, gate, up)
    lanes.round(token, (cot, 2), (up, 2), down)
    lanes.round(token, gate)
    lanes.round(cot, up)
    parts = lanes.drain(gate, up)
    gate_up_full = weave_gate_up(parts, me, s)
    (other_down,) = lanes.drain(down)
    down_full = whole_call(
        pair_kernel,
        jax.ShapeDtypeStruct((padded, D), bf16),
        [core],
        [down_weight, other_down],
    )
    lanes.drain(token, cot)
    early = feed_forward(token_blocks[0], cot_blocks[0], gate_up_full, down_full, f32)
    last = feed_forward(
        [after(token_blocks[1][0], early[5]), token_blocks[1][1]],
        cot_blocks[1],
        gate_up_full,
        down_full,
        bf16,
    )
    back = Move(scatter_tokens(early[5:], last[5:]))
    lanes.round(back)

    half = last[5].shape[0]
    gate_terms = gate_up_grad([early[3], last[3]], [early[1], last[1]], me, s)
    out_terms = [[dot(v[0][:half], down_full), dot(v[0][half:], down_full)] for v in (early, last)]
    gate = Move(unshuffle_part(gate_terms, far + [Z, X], me))
    result = Move(scatter_tokens(out_terms[0], [term.astype(bf16) for term in out_terms[1]]))
    lanes.round(back, gate)
    up_terms = gate_up_grad(
        [early[3], last[3]], [lanes.hold(early[2]), lanes.hold(last[2])], me, s
    )
    up = Move(unshuffle_part(up_terms, [X, Z] + far, me))
    attended_turned = turn_rows(lanes.hold(attended), me, s)
    normed_turned = turn_rows(lanes.hold(normed), me, s)
    lanes.round(back, gate, result, up)
    down_terms = t_dot(lanes.hold(early[0]), early[4]) + t_dot(lanes.hold(last[0]), last[4])
    down_terms = down_terms[:unit].astype(bf16).reshape(2, unit // 2, D)
    down = Move(sum_down(down_terms, core))
    (grad_normed_two,) = lanes.drain(back)
    lanes.round((gate, 2), (up, 2))

    grad_middle, grad_branch, gain_two_part, grad_queries, keep, give = whole_call(
        attend_back_kernel,
        (
            rows_f32,
            rows_bf16,
            jax.ShapeDtypeStruct((1, D), f32),
            rows_bf16,
            jax.ShapeDtypeStruct((tokens, 2 * KW), f32),
            jax.ShapeDtypeStruct((tokens, 2 * KW), bf16),
        ),
        [s],
        [grad_normed_two, middle, gain_two, grad_rows, out_full, queries, kv, other_kv]
        + [ids_col, ids_row, other_row, logs, cosines, sines],
        flops=2 * tokens * D * (D + 20 * tokens),
    )
    other = Move(swap("y", give))
    lanes.more(other)
    (got,) = lanes.drain(other)
    out = Move(scatter_weight(attended_turned, grad_branch, s, 1024))
    grad_projected, input_grad, gain_one_part, bias_part = whole_call(
        project_back_kernel,
        (
            jax.ShapeDtypeStruct((tokens, QW + 2 * KW), bf16),
            rows_f32,
            jax.ShapeDtypeStruct((1, D), f32),
            jax.ShapeDtypeStruct((1, QW + 2 * KW), f32),
        ),
        [s],
        [grad_queries, keep, got, cosines, sines, qkv_full, input_rows, gain_one, grad_middle],
        flops=2 * tokens * D * (QW + 2 * KW),
    )
    lanes.beside(grad_projected)
    qkv = Move(scatter_weight(normed_turned, grad_projected, s, 1280))
    sums = Move(sum_everywhere(join(gain_one_part[0], bias_part[0], gain_two_part[0])))
    lanes.round(qkv, down, result)
    lanes.round(qkv, (result, 2), out, down)
    lanes.round(qkv, gate, up, sums)
    lanes.round(qkv, gate, up, down, sums)
    lanes.round(qkv, out, (up, 2), (gate, 2), sums)
    lanes.round(qkv, out, sums)
    lanes.round(out, up, sums)
    qkv_weight_total, out_weight_total, down_total, out_sum, sums, *parts = lanes.drain(
        qkv, out, down, result, sums, gate, up
    )
    gate_up_total = widen_gate_up(parts, s)
    output = (middle + out_sum).astype(bf16).reshape(inputs.shape)
    width = bias_part.shape[1]
    return (
        output,
        input_grad.reshape(inputs.shape),
        sums[:D],
        qkv_weight_total,
        sums[D : D + width],
        out_weight_total,
        sums[D + width :],
        gate_up_total,
        down_total,
    )


def solution(mesh):
    placed = (
        P("fsdp", "seq", None),
        P("fsdp", "seq"),
        P("fsdp", None),
        P(),
        P("fsdp", None),
        P(),
        P("fsdp", None),
        P(),
        P("fsdp", None),
        P("fsdp", None),
        P("fsdp", "seq", None),
    )
    return jax.shard_map(
        body,
        mesh=mesh,
        in_specs=placed,
        out_specs=(
            P("fsdp", "seq", None),
            P("fsdp", "seq", None),
            P(),
            P("fsdp", None),
            P(),
            P("fsdp", None),
            P(),
            P("fsdp", None),
            P("fsdp", None),
        ),
        check_vma=False,
    )
```

```python
import functools

import jax
import jax.numpy as jnp
from jax import lax
from jax.experimental import pallas as pl
from jax.experimental.pallas import tpu as pltpu
from jax.sharding import PartitionSpec as P

D = 1536
FF = 8960
HQ = 12
KV = 2
HD = 128
GROUP = HQ // KV
QW = HQ * HD
KW = KV * HD

rope_base = 1000000.0
norm_eps = 1e-06
bf16 = jnp.bfloat16
f32 = jnp.float32


CORE, X, Z = 1, 2, 4
ROTATED = ((Z, X, "y"), (X, "y", Z), ("y", Z, X))
CROSSED = ((X, Z), (Z, X))
VMEM = 48 * 1024 * 1024


def far_bits():
    return [bit for bit in (8 << i for i in range(16)) if bit < lax.axis_size("fsdp")]


def after(value, *earlier):
    return lax.optimization_barrier((value,) + earlier)[0]


class Move:
    def __init__(self, steps):
        self.steps = steps
        self.result = self.arrived = None
        self.wanted = next(steps)

    def resume(self, beside=()):
        if self.arrived is None:
            return
        arrived, self.arrived = self.arrived, None
        if beside:
            arrived = [after(value, *beside) for value in arrived]
        try:
            self.wanted = self.steps.send(arrived)
        except StopIteration as stop:
            self.result = stop.value


class Lanes:
    def __init__(self):
        self.flying, self.ended, self.before, self.kernels = [], [], [], []

    def round(self, *entries):
        ended = [value for value, left in self.flying if left <= 1] + self.kernels
        self.before, self.ended = ended + self.ended, ended
        self.flying = [(value, left - 1) for value, left in self.flying if left > 1]
        self.waited, self.kernels = self.kernels, []
        self.more(*entries)

    def more(self, *entries):
        size = lax.axis_size("fsdp")
        for entry in entries:
            move, lasts = entry if isinstance(entry, tuple) else (entry, 1)
            move.resume(self.waited)
            if not move.wanted:
                continue
            move.arrived = []
            for link, value in move.wanted:
                if self.before:
                    value = after(value, *self.before)
                if link == "y":
                    value = lax.ppermute(value, "seq", [(0, 1), (1, 0)])
                else:
                    value = lax.ppermute(value, "fsdp", [(i, i ^ link) for i in range(size)])
                move.arrived.append(value)
                self.flying.append((value, lasts))
            move.wanted = None

    def hold(self, value):
        return after(value, *self.before) if self.before else value

    def beside(self, *values):
        self.kernels += values

    def drain(self, *moves):
        for move in moves:
            move.resume()
        while any(move.wanted for move in moves):
            self.round(*moves)
            for move in moves:
                move.resume()
        return [move.result for move in moves]


def add(left, right):
    return left.astype(f32) + right.astype(f32)


def dot(left, right):
    return jnp.dot(left, right, preferred_element_type=f32)


def dot_t(left, right):
    return lax.dot_general(left, right, (((1,), (1,)), ((), ())), preferred_element_type=f32)


def t_dot(left, right):
    return lax.dot_general(left, right, (((0,), (0,)), ((), ())), preferred_element_type=f32)


def join(*pieces, axis=0):
    return jnp.concatenate(pieces, axis=axis)


def pick(value, index, axis):
    return lax.index_in_dim(value, index, axis, keepdims=False)


def whole_call(kernel, out_shape, scalars, arrays, scratch=(), flops=0):
    outs = out_shape if isinstance(out_shape, (list, tuple)) else [out_shape]
    moved = sum(a.size * a.dtype.itemsize for a in list(arrays) + list(outs))
    spec = pl.BlockSpec(memory_space=pltpu.VMEM)
    return pl.pallas_call(
        kernel,
        out_shape=out_shape,
        in_specs=[pl.BlockSpec(memory_space=pltpu.SMEM)] + [spec] * len(arrays),
        out_specs=jax.tree.map(lambda _: spec, out_shape),
        scratch_shapes=list(scratch),
        compiler_params=pltpu.CompilerParams(vmem_limit_bytes=VMEM),
        cost_estimate=pl.CostEstimate(flops=flops, bytes_accessed=moved, transcendentals=0),
    )(jnp.stack(scalars).astype(jnp.int32), *arrays)


def gather_tokens(rows, blocks):
    state = rows[None]
    for bit in far_bits():
        (got,) = yield [(bit, state)]
        state = join(state, got)
    half, width = rows.shape[0] // 2, rows.shape[1]
    first, second = state[:, :half], state[:, half:]
    got = yield [(Z, first), (X, second)]
    first, second = join(first, got[0]), join(second, got[1])
    blocks.append([v.reshape(-1, width) for v in (first, second)])
    last = yield [(X, first), (Z, second)]
    blocks.append([v.reshape(-1, width) for v in last])


def scatter_tokens(early, last):
    width = last[0].shape[1]
    far = far_bits()
    count = 1 << len(far)
    half = last[0].shape[0] // count // 2
    got = yield [(X, last[0]), (Z, last[1])]
    first = add(early[0], got[0]).reshape(2, count, half, width)
    second = add(early[1], got[1]).reshape(2, count, half, width)
    got = yield [(Z, first[1].astype(bf16)), (X, second[1].astype(bf16))]
    state = join(add(first[0], got[0]), add(second[0], got[1]), axis=1)
    for bit in reversed(far):
        count //= 2
        (got,) = yield [(bit, state[count:].astype(bf16))]
        state = add(state[:count], got)
    return state[0]


def place_kernel(where, *refs):
    out = refs[-1]
    at = 0
    for ref in refs[:-1]:
        for i in range(ref.shape[0]):
            out[where[at]] = ref[i]
            at += 1


def cut_columns(width):
    third = width // 3 // 128 * 128
    return ((0, third), (third, 2 * third), (2 * third, width))


def gather_weight(shard, me, s):
    size = lax.axis_size("fsdp")
    half, width = shard.shape[0] // 2, shard.shape[1]
    state = lax.dynamic_index_in_dim(shard.reshape(2, half, width), s, 0)
    marks = [(0, 0)]
    for bit in far_bits():
        (got,) = yield [(bit, state)]
        state = join(state, got)
        marks = marks + [(f ^ bit, h) for f, h in marks]
    states = [state[:, :, low:high] for low, high in cut_columns(width)]
    for step in range(3):
        got = yield [(ROTATED[part][step], states[part]) for part in range(3)]
        states = [join(*pair) for pair in zip(states, got)]
    turns = []
    for order in ROTATED:
        index = [order.index(link) for link in reversed(ROTATED[0])]
        turns.append([2 - i for i in index])
    count = len(marks)
    split = [v.reshape(2, 2, 2, count, half, v.shape[-1]) for v in states]
    state = join(*[jnp.transpose(v, t + [3, 4, 5]) for v, t in zip(split, turns)], axis=-1)
    state = state.reshape(8 * count, half, width)
    for link in ROTATED[0]:
        marks = marks + [(f, 1 - h) if link == "y" else (f ^ link, h) for f, h in marks]
    (got,) = yield [(CORE, state)]
    where = []
    for core in range(2):
        where += [(me ^ f ^ core) * 2 + (s ^ h) for f, h in marks]
    whole = whole_call(
        place_kernel,
        jax.ShapeDtypeStruct((size * 2, half, width), bf16),
        where,
        [state, got],
    )
    return whole.reshape(size * 2 * half, width)


def gather_weight_plain(shard, me):
    size = lax.axis_size("fsdp")
    rows, width = shard.shape
    state = shard[None]
    marks = [0]
    for bit in far_bits():
        (got,) = yield [(bit, state)]
        state = join(state, got)
        marks = marks + [f ^ bit for f in marks]
    cut = width // 3 // 128 * 128
    first, second = state[:, :, :cut], state[:, :, cut:]
    got = yield [(X, first), (Z, second)]
    first, second = join(first, got[0]), join(second, got[1])
    got = yield [(Z, first), (X, second)]
    count = len(marks)
    second = join(second[:count], got[1][:count], second[count:], got[1][count:])
    state = join(join(first, got[0]), second, axis=2)
    for link in (X, Z):
        marks = marks + [f ^ link for f in marks]
    (got,) = yield [(CORE, state)]
    where = [me ^ f for f in marks] + [me ^ f ^ CORE for f in marks]
    whole = whole_call(
        place_kernel, jax.ShapeDtypeStruct((size, rows, width), bf16), where, [state, got]
    )
    return whole.reshape(size * rows, width)


def order_kernel(where, source, out):
    for i in range(source.shape[0]):
        out[where[i]] = source[i]


def turn_rows(left, me, s):
    size = lax.axis_size("fsdp")
    count = size // 8
    rows = left.shape[1]
    turned = left.T.reshape(size * 2, rows // size // 2, left.shape[0])
    where = []
    for place in range(size):
        for h in range(2):
            k = me ^ place
            kept = ((k % 2) * 2 + (k // 2) % 2) * 2 + (k // 4) % 2
            where.append((kept * count + k // 8) * 2 + (s ^ h))
    return whole_call(
        order_kernel, jax.ShapeDtypeStruct(turned.shape, bf16), where, [turned]
    ).reshape(2, rows // 2, left.shape[0])


def scatter_weight(turned, right, s, cut):
    size = lax.axis_size("fsdp")
    far = far_bits()
    count = 1 << len(far)
    half, width = turned.shape[1] // size, right.shape[1]
    (got,) = yield [(CORE, dot(turned[1], right).astype(bf16))]
    total = add(dot(turned[0], right), got).reshape(2, 2, count, 2, half, width)
    low, high = total[..., :cut], total[..., cut:]
    got = yield [(X, low[1].astype(bf16)), (Z, high[:, 1].astype(bf16))]
    low, high = add(low[0], got[0]), add(high[:, 0], got[1])
    got = yield [(Z, low[1].astype(bf16)), (X, high[1].astype(bf16))]
    state = join(add(low[0], got[0]), add(high[0], got[1]), axis=-1)
    for bit in reversed(far):
        count //= 2
        (got,) = yield [(bit, state[count:].astype(bf16))]
        state = add(state[:count], got)
    mine = state[0].astype(bf16)
    (other,) = yield [("y", mine)]
    near, far_half = add(mine[0], other[1]), add(mine[1], other[0])
    low = jnp.where(s == 0, near, far_half)
    high = jnp.where(s == 0, far_half, near)
    return join(low, high)


def sum_everywhere(value):
    for link in [CORE, X, Z] + far_bits() + ["y"]:
        (got,) = yield [(link, value)]
        value = value + got
    return value


def swap(link, value):
    (got,) = yield [(link, value)]
    return got


def exchange_blocks(blocks, order):
    axes = list(reversed(far_bits())) + [Z, X]
    state = blocks.reshape((1,) + (2,) * len(axes) + blocks.shape[1:])
    marks = [0]
    for link in order:
        axis = 1 + axes.index(link)
        axes.remove(link)
        (got,) = yield [(link, pick(state, 1, axis))]
        state = join(pick(state, 0, axis), got)
        marks = marks + [f ^ link for f in marks]
    return state, marks


def split_kernel(unit, at, shard, gate, up):
    for chip in range(gate.shape[0]):
        low = chip * unit
        gate[at[0] ^ chip] = shard[at[1], :, low : low + unit]
        up[at[0] ^ chip] = shard[at[1], :, FF + low : FF + low + unit]


def weave_kernel(unit, where, *refs):
    out = refs[-1]
    half, padded = out.shape[1:]
    at = 0
    for ref in refs[:-1]:
        for i in range(ref.shape[0]):
            out[where[at], :, :unit] = ref[i]
            if padded > unit:
                out[where[at], :, unit:] = jnp.zeros((half, padded - unit), out.dtype)
            at += 1


def split_gate_up(shard, me, s):
    size = lax.axis_size("fsdp")
    half = shard.shape[0] // 2
    unit = 2 * FF // size
    block = jax.ShapeDtypeStruct((size // 2, half, unit), bf16)
    return whole_call(
        functools.partial(split_kernel, unit),
        (block, block),
        [me // 2, s],
        [shard.reshape(2, half, 2 * FF)],
    )


def shuffle_part(blocks, order):
    mine, marks = yield from exchange_blocks(blocks, order)
    (other,) = yield [("y", mine)]
    (got,) = yield [(CORE, join(mine, other))]
    return [mine, other, got], marks


def weave_part(blocks, marks, me, s):
    size = lax.axis_size("fsdp")
    half, unit = blocks[0].shape[1:]
    padded = -(-unit // 384) * 384
    where = []
    for core in range(2):
        for h in range(2):
            where += [(me ^ f ^ core) * 2 + (s ^ h) for f in marks]
    whole = whole_call(
        functools.partial(weave_kernel, unit),
        jax.ShapeDtypeStruct((size * 2, half, padded), bf16),
        where,
        blocks,
    )
    return whole.reshape(size * 2 * half, padded)


def grad_kernel(count, unit, at, *refs):
    outs = refs[-2:]
    half = outs[0].shape[2]
    total = 0.0
    for j in range(count):
        total = total + t_dot(refs[j][...], refs[count + j][...])
    total = total.astype(bf16)[:, :unit]
    here = total.shape[0] // (2 * half)
    for i in range(here):
        k = at[0] ^ (pl.program_id(0) * here + i)
        for h in range(2):
            low = (2 * i + h) * half
            for core, out in enumerate(outs):

                @pl.when(k % 2 == core)
                def _():
                    out[at[1] ^ h, k // 2] = total[low : low + half]


def gate_up_grad(token_blocks, grad_blocks, me, s):
    size = lax.axis_size("fsdp")
    unit = 2 * FF // size
    padded = grad_blocks[0].shape[1]
    half = D // size // 2
    count = len(token_blocks)
    rows = token_blocks[0].shape[0]
    tile = 768
    return pl.pallas_call(
        functools.partial(grad_kernel, count, unit),
        out_shape=[jax.ShapeDtypeStruct((2, size // 2, half, unit), bf16)] * 2,
        grid=(D // tile,),
        in_specs=[pl.BlockSpec(memory_space=pltpu.SMEM)]
        + [pl.BlockSpec((rows, tile), lambda i: (0, i))] * count
        + [pl.BlockSpec((rows, padded), lambda i: (0, 0))] * count,
        out_specs=[pl.BlockSpec(memory_space=pltpu.VMEM)] * 2,
        compiler_params=pltpu.CompilerParams(vmem_limit_bytes=VMEM),
        cost_estimate=pl.CostEstimate(
            flops=2 * count * rows * D * padded,
            bytes_accessed=2 * count * rows * (D + padded) + 4 * D * unit,
            transcendentals=0,
        ),
    )(jnp.stack([me, s]).astype(jnp.int32), *token_blocks, *grad_blocks)


def spread_kernel(unit, where, blocks, out, held):
    for i in range(blocks.shape[0]):
        held[where[i]] = blocks[i]
    for chip in range(blocks.shape[0]):
        out[:, chip * unit : (chip + 1) * unit] = held[chip]


def widen_kernel(at, gate, up, other_gate, other_up, out):
    for ref, other, low in ((gate, other_gate, 0), (up, other_up, FF)):
        out[at[0], :, low : low + FF] = ref[...].astype(f32)
        out[1 - at[0], :, low : low + FF] = other[...].astype(f32)


def unshuffle_part(terms, order, me):
    half, unit = terms[0].shape[2:]
    (got,) = yield [(CORE, terms[1])]
    total = add(terms[0], got)
    (got,) = yield [("y", total[1].astype(bf16))]
    total = add(total[0], got).astype(bf16)
    blocks, marks = yield from exchange_blocks(total, order)
    mine = whole_call(
        functools.partial(spread_kernel, unit),
        jax.ShapeDtypeStruct((half, FF), bf16),
        [(me ^ f) // 2 for f in marks],
        [blocks],
        scratch=[pltpu.VMEM(blocks.shape, bf16)],
    )
    (other,) = yield [("y", mine)]
    return mine, other


def widen_gate_up(parts, s):
    mine, others = zip(*parts)
    half = mine[0].shape[0]
    whole = whole_call(
        widen_kernel,
        jax.ShapeDtypeStruct((2, half, 2 * FF), f32),
        [s],
        list(mine) + list(others),
    )
    return whole.reshape(2 * half, 2 * FF)


def sum_down(terms, core):
    give = lax.dynamic_index_in_dim(terms, 1 - core, 0, keepdims=False)
    (got,) = yield [(CORE, give)]
    part = add(lax.dynamic_index_in_dim(terms, core, 0, keepdims=False), got).astype(bf16)
    half = part.shape[0] // 2
    (low,) = yield [("y", part[:half])]
    (high,) = yield [("y", part[half:])]
    return add(part, join(low, high))


def rope_tables(positions):
    steps_half = jnp.arange(HD // 2, dtype=f32)
    inverse = rope_base ** (-2.0 * steps_half / HD)
    angles = positions.astype(f32)[:, None] * inverse
    cosines, sines = jnp.cos(angles), jnp.sin(angles)
    return join(cosines, cosines, axis=1), join(-sines, sines, axis=1)


def turn(head, cosines, sines):
    return head * cosines + pltpu.roll(head, HD // 2, 1) * sines


def rms_scale(values):
    return lax.rsqrt(jnp.mean(values * values, axis=-1, keepdims=True) + norm_eps)


def norm_backward(grad_normed, values, gain):
    scale_rows = rms_scale(values)
    scaled = grad_normed * gain
    gain_part = jnp.sum(grad_normed * values * scale_rows, axis=0, keepdims=True)
    grad_values = scale_rows * scaled - values * scale_rows**3 * jnp.mean(
        scaled * values, axis=-1, keepdims=True
    )
    return grad_values, gain_part


def head_at(index):
    return slice(index * HD, (index + 1) * HD)


def masks(second, ids_col, ids_row, other_row):
    shape = (ids_col.shape[0], ids_row.shape[1])
    rows = lax.broadcasted_iota(jnp.int32, shape, 0)
    cols = lax.broadcasted_iota(jnp.int32, shape, 1)
    near = (ids_col[...] == ids_row[...]) & (rows >= cols)
    far = (ids_col[...] == other_row[...]) & (rows + shape[0] * second >= shape[0])
    return near, far


def project_kernel(at, inputs, gain, weight, bias, cosines, sines, normed, queries, kv):
    values = inputs[...].astype(f32)
    rows = (values * rms_scale(values) * gain[...]).astype(bf16)
    normed[...] = rows
    projected = dot(rows, weight[...]) + bias[...]
    cos, sin = cosines[...], sines[...]
    for head in range(HQ):
        queries[:, head_at(head)] = turn(projected[:, head_at(head)], cos, sin).astype(bf16)
    for head in range(KV):
        kv[:, head_at(head)] = turn(projected[:, head_at(HQ + head)], cos, sin).astype(bf16)
    kv[:, KW:] = projected[:, QW + KW :].astype(bf16)


def attend_kernel(
    at, inputs, queries, kv, other, ids_col, ids_row, other_row, weight, gain,
    attended, logs, middle, normed,
):
    near, far = masks(at[0], ids_col, ids_row, other_row)
    factor = HD ** (-0.5)
    lanes = lax.broadcasted_iota(jnp.int32, logs.shape, 1)
    kept = jnp.zeros(logs.shape, f32)
    for head in range(HQ):
        k, v = head_at(head // GROUP), head_at(KV + head // GROUP)
        q = queries[:, head_at(head)]
        first = jnp.where(near, dot_t(q, kv[:, k]) * factor, -1e30)
        second = jnp.where(far, dot_t(q, other[:, k]) * factor, -1e30)
        peak = jnp.maximum(
            jnp.max(first, axis=-1, keepdims=True), jnp.max(second, axis=-1, keepdims=True)
        )
        total = jnp.sum(jnp.exp(first - peak), axis=-1, keepdims=True)
        total = total + jnp.sum(jnp.exp(second - peak), axis=-1, keepdims=True)
        log_total = peak + jnp.log(total)
        kept = jnp.where(lanes == head, log_total, kept)
        out = dot(jnp.exp(first - log_total).astype(bf16), kv[:, v])
        out = out + dot(jnp.exp(second - log_total).astype(bf16), other[:, v])
        attended[:, head_at(head)] = out.astype(bf16)
    logs[...] = kept
    rows = inputs[...].astype(f32) + dot(attended[...], weight[...])
    middle[...] = rows
    normed[...] = (rows * rms_scale(rows) * gain[...]).astype(bf16)


def attend_back_kernel(
    at, grad_normed, middle, gain, cotangent, weight, queries, kv, other,
    ids_col, ids_row, other_row, logs, cosines, sines,
    grad_middle, grad_branch, gain_part, grad_queries, keep, give,
):
    grad_values, part = norm_backward(grad_normed[...], middle[...], gain[...])
    gain_part[...] = part
    grad_rows = cotangent[...].astype(f32) + grad_values
    grad_middle[...] = grad_rows
    branch = grad_rows.astype(bf16)
    grad_branch[...] = branch
    grad_out = dot_t(branch, weight[...]).astype(bf16)
    near, far = masks(at[0], ids_col, ids_row, other_row)
    factor = HD ** (-0.5)
    lanes = lax.broadcasted_iota(jnp.int32, logs.shape, 1)
    cos, sin = cosines[...], -sines[...]
    for group in range(KV):
        k, v = head_at(group), head_at(KV + group)
        sums = [jnp.zeros((kv.shape[0], HD), f32) for _ in range(4)]
        for head in range(group * GROUP, (group + 1) * GROUP):
            q, g = queries[:, head_at(head)], grad_out[:, head_at(head)]
            log_total = jnp.sum(
                jnp.where(lanes == head, logs[...], 0.0), axis=-1, keepdims=True
            )
            first = jnp.where(near, dot_t(q, kv[:, k]) * factor, -1e30)
            second = jnp.where(far, dot_t(q, other[:, k]) * factor, -1e30)
            first, second = jnp.exp(first - log_total), jnp.exp(second - log_total)
            grad_first, grad_second = dot_t(g, kv[:, v]), dot_t(g, other[:, v])
            balance = jnp.sum(first * grad_first, axis=-1, keepdims=True)
            balance = balance + jnp.sum(second * grad_second, axis=-1, keepdims=True)
            grad_first = (first * (grad_first - balance)).astype(bf16)
            grad_second = (second * (grad_second - balance)).astype(bf16)
            grad_q = (dot(grad_first, kv[:, k]) + dot(grad_second, other[:, k])) * factor
            grad_q = turn(grad_q.astype(bf16).astype(f32), cos, sin)
            grad_queries[:, head_at(head)] = grad_q.astype(bf16)
            sums[0] = sums[0] + t_dot(grad_first, q)
            sums[1] = sums[1] + t_dot(first.astype(bf16), g)
            sums[2] = sums[2] + t_dot(grad_second, q)
            sums[3] = sums[3] + t_dot(second.astype(bf16), g)
        keep[:, k] = sums[0] * factor
        keep[:, v] = sums[1]
        give[:, k] = (sums[2] * factor).astype(bf16)
        give[:, v] = sums[3].astype(bf16)


def project_back_kernel(
    at, grad_queries, keep, got, cosines, sines, weight, inputs, gain, grad_middle,
    grad_projected, input_grad, gain_part, bias_part,
):
    grad_kv = (keep[...] + got[...].astype(f32)).astype(bf16)
    cos, sin = cosines[...], -sines[...]
    grad_projected[:, :QW] = grad_queries[...]
    for head in range(KV):
        grad_k = turn(grad_kv[:, head_at(head)].astype(f32), cos, sin)
        grad_projected[:, head_at(HQ + head)] = grad_k.astype(bf16)
    grad_projected[:, QW + KW :] = grad_kv[:, KW:]
    rows = grad_projected[...]
    bias_part[...] = jnp.sum(rows.astype(f32), axis=0, keepdims=True)
    grad_normed = dot_t(rows, weight[...])
    grad_values, part = norm_backward(grad_normed, inputs[...].astype(f32), gain[...])
    gain_part[...] = part
    input_grad[...] = grad_middle[...] + grad_values


def feed_kernel(
    tokens_a, tokens_b, cot_a, cot_b, gate_weight, up_weight, down_weight,
    hidden, grad_gate, grad_up, tokens, cotangent, back_a, back_b, total,
):
    step, steps = pl.program_id(0), pl.num_programs(0)
    half = tokens_a.shape[0]

    @pl.when(step == 0)
    def _():
        tokens[:half], tokens[half:] = tokens_a[...], tokens_b[...]
        cotangent[:half], cotangent[half:] = cot_a[...], cot_b[...]
        total[...] = jnp.zeros_like(total)

    gate = dot(tokens[...], gate_weight[...])
    up = dot(tokens[...], up_weight[...])
    grad_hidden = dot_t(cotangent[...], down_weight[...])
    sigmoid = jax.nn.sigmoid(gate)
    silu = gate * sigmoid
    hidden[...] = (silu * up).astype(bf16)
    gate_rows = (grad_hidden * up * sigmoid * (1.0 + gate * (1.0 - sigmoid))).astype(bf16)
    up_rows = (grad_hidden * silu).astype(bf16)
    grad_gate[...] = gate_rows
    grad_up[...] = up_rows
    total[...] += dot_t(
        join(gate_rows, up_rows, axis=1), join(gate_weight[...], up_weight[...], axis=1)
    )

    @pl.when(step == steps - 1)
    def _():
        back_a[...] = total[:half].astype(back_a.dtype)
        back_b[...] = total[half:].astype(back_b.dtype)


def feed_forward(tokens, cotangent, gate_up_weight, down_weight, back_type):
    half = tokens[0].shape[0]
    if half > 256 and half % 256 == 0:
        parts = [
            feed_forward(
                [v[low : low + 256] for v in tokens],
                [v[low : low + 256] for v in cotangent],
                gate_up_weight,
                down_weight,
                back_type,
            )
            for low in range(0, half, 256)
        ]
        halves = [
            join(*[part[i][low : low + 256] for low in (0, 256) for part in parts])
            for i in range(5)
        ]
        return (*halves, *[join(*[part[i] for part in parts]) for i in (5, 6)])
    rows = 2 * half
    padded = down_weight.shape[0]
    tile = 384
    steps = padded // tile
    whole = pl.BlockSpec((rows, D), lambda j: (0, 0))
    piece = pl.BlockSpec((half, D), lambda j: (0, 0))
    part = pl.BlockSpec((rows, tile), lambda j: (0, j))
    units = jax.ShapeDtypeStruct((rows, padded), bf16)
    lines = jax.ShapeDtypeStruct((rows, D), bf16)
    back = jax.ShapeDtypeStruct((half, D), back_type)
    return pl.pallas_call(
        feed_kernel,
        grid=(steps,),
        out_shape=(units, units, units, lines, lines, back, back),
        in_specs=[piece] * 4
        + [
            pl.BlockSpec((D, tile), lambda j: (0, j)),
            pl.BlockSpec((D, tile), lambda j: (0, j)),
            pl.BlockSpec((tile, D), lambda j: (j, 0)),
        ],
        out_specs=(part, part, part, whole, whole, piece, piece),
        scratch_shapes=[pltpu.VMEM((rows, D), f32)],
        compiler_params=pltpu.CompilerParams(vmem_limit_bytes=VMEM),
        cost_estimate=pl.CostEstimate(
            flops=10 * rows * D * padded,
            bytes_accessed=6 * D * padded + 8 * rows * D + 6 * rows * padded,
            transcendentals=rows * padded,
        ),
    )(*tokens, *cotangent, *gate_up_weight, down_weight)


def pair_kernel(at, own, other, out):
    rows = own.shape[0]
    for core, first, second in ((0, own, other), (1, other, own)):

        @pl.when(at[0] == core)
        def _():
            out[:rows], out[rows : 2 * rows] = first[...], second[...]

    if out.shape[0] > 2 * rows:
        out[2 * rows :] = jnp.zeros((out.shape[0] - 2 * rows, out.shape[1]), out.dtype)


def body(
    inputs,
    positions,
    segments,
    gain_one,
    qkv_weight,
    qkv_bias,
    out_weight,
    gain_two,
    gate_up_weight,
    down_weight,
    cotangent,
):
    tokens = inputs.shape[0] * inputs.shape[1]
    size = lax.axis_size("fsdp")
    me = lax.axis_index("fsdp")
    s = lax.axis_index("seq")
    unit = 2 * FF // size
    padded = -(-unit // 384) * 384

    lanes = Lanes()
    far = far_bits()
    core = me % 2
    input_rows = inputs.reshape(tokens, D)
    grad_rows = cotangent.reshape(tokens, D)
    gate_blocks, up_blocks = split_gate_up(gate_up_weight, me, s)
    cot_blocks, token_blocks = [], []
    qkv = Move(gather_weight(qkv_weight, me, s))
    out = Move(gather_weight_plain(out_weight, me))
    gate = Move(shuffle_part(gate_blocks, [X, *far, Z]))
    up = Move(shuffle_part(up_blocks, [X, *far, Z]))
    cot = Move(gather_tokens(grad_rows, cot_blocks))
    down = Move(swap(CORE, down_weight))
    lanes.round(qkv, (up, 2))
    lanes.round(qkv, (out, 2))
    lanes.round(qkv, gate)
    lanes.round(qkv, out, (gate, 2))
    lanes.round(qkv, out)
    (qkv_full,) = lanes.drain(qkv)

    rows_bf16 = jax.ShapeDtypeStruct((tokens, D), bf16)
    rows_f32 = jax.ShapeDtypeStruct((tokens, D), f32)
    cosines, sines = rope_tables(positions.reshape(tokens))
    ids = segments.reshape(2, tokens)
    ids_row = lax.dynamic_index_in_dim(ids, s, 0)
    other_row = lax.dynamic_index_in_dim(ids, 1 - s, 0)
    ids_col = ids_row.reshape(tokens, 1)
    gain_one, gain_two = gain_one[None], gain_two[None]
    normed, queries, kv = whole_call(
        project_kernel,
        (rows_bf16, rows_bf16, jax.ShapeDtypeStruct((tokens, 2 * KW), bf16)),
        [s],
        [input_rows, gain_one, qkv_full, qkv_bias[None], cosines, sines],
        flops=2 * tokens * D * (QW + 2 * KW),
    )
    lanes.beside(kv)
    other = Move(swap("y", kv))
    lanes.round(other, out, (up, 2), gate)
    other_kv, out_full = lanes.drain(other, out)
    attended, logs, middle, normed_two = whole_call(
        attend_kernel,
        (rows_bf16, jax.ShapeDtypeStruct((tokens, HD), f32), rows_f32, rows_bf16),
        [s],
        [input_rows, queries, kv, other_kv, ids_col, ids_row, other_row, out_full, gain_two],
        flops=2 * tokens * D * (D + 8 * tokens),
    )

    lanes.beside(normed_two)
    token = Move(gather_tokens(normed_two, token_blocks))
    lanes.round(token, gate, up)
    lanes.round(down, (up, 2), (cot, 2))
    lanes.round(token, (gate, 3))
    lanes.round(cot, up)
    parts = lanes.drain(gate, up)
    gate_full, up_full = [weave_part(*part, me, s) for part in parts]
    (other_down,) = lanes.drain(down)
    down_full = whole_call(
        pair_kernel,
        jax.ShapeDtypeStruct((padded, D), bf16),
        [core],
        [down_weight, other_down],
    )
    lanes.drain(token, cot)
    early = feed_forward(token_blocks[0], cot_blocks[0], (gate_full, up_full), down_full, f32)
    last = feed_forward(
        [after(token_blocks[1][0], early[5]), token_blocks[1][1]],
        cot_blocks[1],
        (gate_full, up_full),
        down_full,
        bf16,
    )
    back = Move(scatter_tokens(early[5:], last[5:]))
    lanes.round(back)

    half = last[5].shape[0]
    gate_terms = gate_up_grad([early[3], last[3]], [early[1], last[1]], me, s)
    out_terms = [[dot(v[0][:half], down_full), dot(v[0][half:], down_full)] for v in (early, last)]
    gate = Move(unshuffle_part(gate_terms, [*far, Z, X], me))
    result = Move(scatter_tokens(out_terms[0], [term.astype(bf16) for term in out_terms[1]]))
    lanes.round(back, gate)
    up_terms = gate_up_grad(
        [early[3], last[3]], [lanes.hold(early[2]), lanes.hold(last[2])], me, s
    )
    up = Move(unshuffle_part(up_terms, [X, Z, *far], me))
    attended_turned = turn_rows(lanes.hold(attended), me, s)
    normed_turned = turn_rows(lanes.hold(normed), me, s)
    lanes.round(back, gate, result, up)
    down_terms = t_dot(lanes.hold(early[0]), early[4]) + t_dot(lanes.hold(last[0]), last[4])
    down_terms = down_terms[:unit].astype(bf16).reshape(2, unit // 2, D)
    down = Move(sum_down(down_terms, core))
    (grad_normed_two,) = lanes.drain(back)
    lanes.round((gate, 2), (up, 2))

    grad_middle, grad_branch, gain_two_part, grad_queries, keep, give = whole_call(
        attend_back_kernel,
        (
            rows_f32,
            rows_bf16,
            jax.ShapeDtypeStruct((1, D), f32),
            rows_bf16,
            jax.ShapeDtypeStruct((tokens, 2 * KW), f32),
            jax.ShapeDtypeStruct((tokens, 2 * KW), bf16),
        ),
        [s],
        [grad_normed_two, middle, gain_two, grad_rows, out_full, queries, kv, other_kv]
        + [ids_col, ids_row, other_row, logs, cosines, sines],
        flops=2 * tokens * D * (D + 20 * tokens),
    )
    other = Move(swap("y", give))
    lanes.more(other)
    (got,) = lanes.drain(other)
    out = Move(scatter_weight(attended_turned, grad_branch, s, 1024))
    grad_projected, input_grad, gain_one_part, bias_part = whole_call(
        project_back_kernel,
        (
            jax.ShapeDtypeStruct((tokens, QW + 2 * KW), bf16),
            rows_f32,
            jax.ShapeDtypeStruct((1, D), f32),
            jax.ShapeDtypeStruct((1, QW + 2 * KW), f32),
        ),
        [s],
        [grad_queries, keep, got, cosines, sines, qkv_full, input_rows, gain_one, grad_middle],
        flops=2 * tokens * D * (QW + 2 * KW),
    )
    lanes.beside(grad_projected)
    qkv = Move(scatter_weight(normed_turned, grad_projected, s, 1280))
    sums = Move(sum_everywhere(join(gain_one_part[0], bias_part[0], gain_two_part[0])))
    lanes.round(qkv, down, result)
    lanes.round(qkv, (result, 2), out, down)
    lanes.round(qkv, gate, up, sums)
    lanes.round(qkv, gate, up, down, sums)
    lanes.round(qkv, out, (up, 2), (gate, 2), sums)
    lanes.round(qkv, out, sums)
    lanes.round(out, up, sums)
    qkv_weight_total, out_weight_total, down_total, out_sum, sums, *parts = lanes.drain(
        qkv, out, down, result, sums, gate, up
    )
    gate_up_total = widen_gate_up(parts, s)
    output = (middle + out_sum).astype(bf16).reshape(inputs.shape)
    width = bias_part.shape[1]
    return (
        output,
        input_grad.reshape(inputs.shape),
        sums[:D],
        qkv_weight_total,
        sums[D : D + width],
        out_weight_total,
        sums[D + width :],
        gate_up_total,
        down_total,
    )


def solution(mesh):
    placed = (
        P("fsdp", "seq", None),
        P("fsdp", "seq"),
        P("fsdp", None),
        P(),
        P("fsdp", None),
        P(),
        P("fsdp", None),
        P(),
        P("fsdp", None),
        P("fsdp", None),
        P("fsdp", "seq", None),
    )
    return jax.shard_map(
        body,
        mesh=mesh,
        in_specs=placed,
        out_specs=(
            P("fsdp", "seq", None),
            P("fsdp", "seq", None),
            P(),
            P("fsdp", None),
            P(),
            P("fsdp", None),
            P(),
            P("fsdp", None),
            P("fsdp", None),
        ),
        check_vma=False,
    )
```

```python
import functools

import jax
import jax.numpy as jnp
from jax import lax
from jax.experimental import pallas as pl
from jax.experimental.pallas import tpu as pltpu
from jax.sharding import PartitionSpec as P

D = 1536
FF = 8960
HQ = 12
KV = 2
HD = 128
GROUP = HQ // KV
QW = HQ * HD
KW = KV * HD

rope_base = 1000000.0
norm_eps = 1e-06
bf16 = jnp.bfloat16
f32 = jnp.float32


CORE, X, Z = 1, 2, 4
ROTATED = ((Z, X, "y"), (X, "y", Z), ("y", Z, X))
CROSSED = ((X, Z), (Z, X))
VMEM = 48 * 1024 * 1024


def far_bits():
    return [bit for bit in (8 << i for i in range(16)) if bit < lax.axis_size("fsdp")]


def after(value, *earlier):
    return lax.optimization_barrier((value,) + earlier)[0]


class Move:
    def __init__(self, steps):
        self.steps = steps
        self.result = self.arrived = None
        self.wanted = next(steps)

    def resume(self, beside=()):
        if self.arrived is None:
            return
        arrived, self.arrived = self.arrived, None
        if beside:
            arrived = [after(value, *beside) for value in arrived]
        try:
            self.wanted = self.steps.send(arrived)
        except StopIteration as stop:
            self.result = stop.value


class Lanes:
    def __init__(self):
        self.flying, self.ended, self.before, self.kernels = [], [], [], []

    def round(self, *entries):
        ended = [value for value, left in self.flying if left <= 1] + self.kernels
        self.before, self.ended = ended + self.ended, ended
        self.flying = [(value, left - 1) for value, left in self.flying if left > 1]
        self.waited, self.kernels = self.kernels, []
        self.more(*entries)

    def more(self, *entries):
        size = lax.axis_size("fsdp")
        for entry in entries:
            move, lasts = entry if isinstance(entry, tuple) else (entry, 1)
            move.resume(self.waited)
            if not move.wanted:
                continue
            move.arrived = []
            for link, value in move.wanted:
                if self.before:
                    value = after(value, *self.before)
                if link == "y":
                    value = lax.ppermute(value, "seq", [(0, 1), (1, 0)])
                else:
                    value = lax.ppermute(value, "fsdp", [(i, i ^ link) for i in range(size)])
                move.arrived.append(value)
                self.flying.append((value, lasts))
            move.wanted = None

    def hold(self, value):
        return after(value, *self.before) if self.before else value

    def beside(self, *values):
        self.kernels += values

    def drain(self, *moves):
        for move in moves:
            move.resume()
        while any(move.wanted for move in moves):
            self.round(*moves)
            for move in moves:
                move.resume()
        return [move.result for move in moves]


def add(left, right):
    return left.astype(f32) + right.astype(f32)


def dot(left, right):
    return jnp.dot(left, right, preferred_element_type=f32)


def dot_t(left, right):
    return lax.dot_general(left, right, (((1,), (1,)), ((), ())), preferred_element_type=f32)


def t_dot(left, right):
    return lax.dot_general(left, right, (((0,), (0,)), ((), ())), preferred_element_type=f32)


def join(*pieces, axis=0):
    return jnp.concatenate(pieces, axis=axis)


def pick(value, index, axis):
    return lax.index_in_dim(value, index, axis, keepdims=False)


def whole_call(kernel, out_shape, scalars, arrays, scratch=(), flops=0):
    outs = out_shape if isinstance(out_shape, (list, tuple)) else [out_shape]
    moved = sum(a.size * a.dtype.itemsize for a in list(arrays) + list(outs))
    spec = pl.BlockSpec(memory_space=pltpu.VMEM)
    return pl.pallas_call(
        kernel,
        out_shape=out_shape,
        in_specs=[pl.BlockSpec(memory_space=pltpu.SMEM)] + [spec] * len(arrays),
        out_specs=jax.tree.map(lambda _: spec, out_shape),
        scratch_shapes=list(scratch),
        compiler_params=pltpu.CompilerParams(vmem_limit_bytes=VMEM),
        cost_estimate=pl.CostEstimate(flops=flops, bytes_accessed=moved, transcendentals=0),
    )(jnp.stack(scalars).astype(jnp.int32), *arrays)


def gather_tokens(rows, blocks):
    state = rows[None]
    for bit in far_bits():
        (got,) = yield [(bit, state)]
        state = join(state, got)
    half, width = rows.shape[0] // 2, rows.shape[1]
    first, second = state[:, :half], state[:, half:]
    got = yield [(Z, first), (X, second)]
    first, second = join(first, got[0]), join(second, got[1])
    blocks.append([v.reshape(-1, width) for v in (first, second)])
    last = yield [(X, first), (Z, second)]
    blocks.append([v.reshape(-1, width) for v in last])


def scatter_tokens(early, last):
    width = last[0].shape[1]
    far = far_bits()
    count = 1 << len(far)
    half = last[0].shape[0] // count // 2
    got = yield [(X, last[0]), (Z, last[1])]
    first = add(early[0], got[0]).reshape(2, count, half, width)
    second = add(early[1], got[1]).reshape(2, count, half, width)
    got = yield [(Z, first[1].astype(bf16)), (X, second[1].astype(bf16))]
    state = join(add(first[0], got[0]), add(second[0], got[1]), axis=1)
    for bit in reversed(far):
        count //= 2
        (got,) = yield [(bit, state[count:].astype(bf16))]
        state = add(state[:count], got)
    return state[0]


def place_kernel(where, *refs):
    out = refs[-1]
    at = 0
    for ref in refs[:-1]:
        for i in range(ref.shape[0]):
            out[where[at]] = ref[i]
            at += 1


def cut_columns(width):
    third = width // 3 // 128 * 128
    return ((0, third), (third, 2 * third), (2 * third, width))


def gather_weight(shard, me, s):
    size = lax.axis_size("fsdp")
    half, width = shard.shape[0] // 2, shard.shape[1]
    state = lax.dynamic_index_in_dim(shard.reshape(2, half, width), s, 0)
    marks = [(0, 0)]
    for bit in far_bits():
        (got,) = yield [(bit, state)]
        state = join(state, got)
        marks = marks + [(f ^ bit, h) for f, h in marks]
    states = [state[:, :, low:high] for low, high in cut_columns(width)]
    for step in range(3):
        got = yield [(ROTATED[part][step], states[part]) for part in range(3)]
        states = [join(*pair) for pair in zip(states, got)]
    turns = []
    for order in ROTATED:
        index = [order.index(link) for link in reversed(ROTATED[0])]
        turns.append([2 - i for i in index])
    count = len(marks)
    split = [v.reshape(2, 2, 2, count, half, v.shape[-1]) for v in states]
    state = join(*[jnp.transpose(v, t + [3, 4, 5]) for v, t in zip(split, turns)], axis=-1)
    state = state.reshape(8 * count, half, width)
    for link in ROTATED[0]:
        marks = marks + [(f, 1 - h) if link == "y" else (f ^ link, h) for f, h in marks]
    (got,) = yield [(CORE, state)]
    where = []
    for core in range(2):
        where += [(me ^ f ^ core) * 2 + (s ^ h) for f, h in marks]
    whole = whole_call(
        place_kernel,
        jax.ShapeDtypeStruct((size * 2, half, width), bf16),
        where,
        [state, got],
    )
    return whole.reshape(size * 2 * half, width)


def gather_weight_plain(shard, me):
    size = lax.axis_size("fsdp")
    rows, width = shard.shape
    state = shard[None]
    marks = [0]
    for bit in far_bits():
        (got,) = yield [(bit, state)]
        state = join(state, got)
        marks = marks + [f ^ bit for f in marks]
    cut = width // 3 // 128 * 128
    first, second = state[:, :, :cut], state[:, :, cut:]
    got = yield [(X, first), (Z, second)]
    first, second = join(first, got[0]), join(second, got[1])
    got = yield [(Z, first), (X, second)]
    count = len(marks)
    second = join(second[:count], got[1][:count], second[count:], got[1][count:])
    state = join(join(first, got[0]), second, axis=2)
    for link in (X, Z):
        marks = marks + [f ^ link for f in marks]
    (got,) = yield [(CORE, state)]
    where = [me ^ f for f in marks] + [me ^ f ^ CORE for f in marks]
    whole = whole_call(
        place_kernel, jax.ShapeDtypeStruct((size, rows, width), bf16), where, [state, got]
    )
    return whole.reshape(size * rows, width)


def order_kernel(where, source, out):
    for i in range(source.shape[0]):
        out[where[i]] = source[i]


def turn_rows(left, me, s):
    size = lax.axis_size("fsdp")
    count = size // 8
    rows = left.shape[1]
    turned = left.T.reshape(size * 2, rows // size // 2, left.shape[0])
    where = []
    for place in range(size):
        for h in range(2):
            k = me ^ place
            kept = ((k % 2) * 2 + (k // 2) % 2) * 2 + (k // 4) % 2
            where.append((kept * count + k // 8) * 2 + (s ^ h))
    return whole_call(
        order_kernel, jax.ShapeDtypeStruct(turned.shape, bf16), where, [turned]
    ).reshape(2, rows // 2, left.shape[0])


def scatter_weight(turned, right, s, cut):
    size = lax.axis_size("fsdp")
    far = far_bits()
    count = 1 << len(far)
    half, width = turned.shape[1] // size, right.shape[1]
    (got,) = yield [(CORE, dot(turned[1], right).astype(bf16))]
    total = add(dot(turned[0], right), got).reshape(2, 2, count, 2, half, width)
    low, high = total[..., :cut], total[..., cut:]
    got = yield [(X, low[1].astype(bf16)), (Z, high[:, 1].astype(bf16))]
    low, high = add(low[0], got[0]), add(high[:, 0], got[1])
    got = yield [(Z, low[1].astype(bf16)), (X, high[1].astype(bf16))]
    state = join(add(low[0], got[0]), add(high[0], got[1]), axis=-1)
    for bit in reversed(far):
        count //= 2
        (got,) = yield [(bit, state[count:].astype(bf16))]
        state = add(state[:count], got)
    mine = state[0].astype(bf16)
    (other,) = yield [("y", mine)]
    near, far_half = add(mine[0], other[1]), add(mine[1], other[0])
    low = jnp.where(s == 0, near, far_half)
    high = jnp.where(s == 0, far_half, near)
    return join(low, high)


def sum_everywhere(value):
    for link in [CORE, X, Z] + far_bits() + ["y"]:
        (got,) = yield [(link, value)]
        value = value + got
    return value


def swap(link, value):
    (got,) = yield [(link, value)]
    return got


def exchange_blocks(blocks, order):
    axes = list(reversed(far_bits())) + [Z, X]
    state = blocks.reshape((1,) + (2,) * len(axes) + blocks.shape[1:])
    marks = [0]
    for link in order:
        axis = 1 + axes.index(link)
        axes.remove(link)
        (got,) = yield [(link, pick(state, 1, axis))]
        state = join(pick(state, 0, axis), got)
        marks = marks + [f ^ link for f in marks]
    return state, marks


def split_kernel(unit, at, shard, gate, up):
    for chip in range(gate.shape[0]):
        low = chip * unit
        gate[at[0] ^ chip] = shard[at[1], :, low : low + unit]
        up[at[0] ^ chip] = shard[at[1], :, FF + low : FF + low + unit]


def weave_kernel(unit, where, *refs):
    out = refs[-1]
    half, padded = out.shape[1:]
    at = 0
    for ref in refs[:-1]:
        for i in range(ref.shape[0]):
            out[where[at], :, :unit] = ref[i]
            if padded > unit:
                out[where[at], :, unit:] = jnp.zeros((half, padded - unit), out.dtype)
            at += 1


def split_gate_up(shard, me, s):
    size = lax.axis_size("fsdp")
    half = shard.shape[0] // 2
    unit = 2 * FF // size
    block = jax.ShapeDtypeStruct((size // 2, half, unit), bf16)
    return whole_call(
        functools.partial(split_kernel, unit),
        (block, block),
        [me // 2, s],
        [shard.reshape(2, half, 2 * FF)],
    )


def shuffle_part(blocks, order):
    mine, marks = yield from exchange_blocks(blocks, order)
    (other,) = yield [("y", mine)]
    (got,) = yield [(CORE, join(mine, other))]
    return [mine, other, got], marks


def weave_part(blocks, marks, me, s):
    size = lax.axis_size("fsdp")
    half, unit = blocks[0].shape[1:]
    padded = -(-unit // 384) * 384
    where = []
    for core in range(2):
        for h in range(2):
            where += [(me ^ f ^ core) * 2 + (s ^ h) for f in marks]
    whole = whole_call(
        functools.partial(weave_kernel, unit),
        jax.ShapeDtypeStruct((size * 2, half, padded), bf16),
        where,
        blocks,
    )
    return whole.reshape(size * 2 * half, padded)


def grad_kernel(count, unit, at, *refs):
    outs = refs[-2:]
    half = outs[0].shape[2]
    total = 0.0
    for j in range(count):
        total = total + t_dot(refs[j][...], refs[count + j][...])
    total = total.astype(bf16)[:, :unit]
    here = total.shape[0] // (2 * half)
    for i in range(here):
        k = at[0] ^ (pl.program_id(0) * here + i)
        for h in range(2):
            low = (2 * i + h) * half
            for core, out in enumerate(outs):

                @pl.when(k % 2 == core)
                def _():
                    out[at[1] ^ h, k // 2] = total[low : low + half]


def gate_up_grad(token_blocks, grad_blocks, me, s):
    size = lax.axis_size("fsdp")
    unit = 2 * FF // size
    padded = grad_blocks[0].shape[1]
    half = D // size // 2
    count = len(token_blocks)
    rows = token_blocks[0].shape[0]
    tile = 768
    return pl.pallas_call(
        functools.partial(grad_kernel, count, unit),
        out_shape=[jax.ShapeDtypeStruct((2, size // 2, half, unit), bf16)] * 2,
        grid=(D // tile,),
        in_specs=[pl.BlockSpec(memory_space=pltpu.SMEM)]
        + [pl.BlockSpec((rows, tile), lambda i: (0, i))] * count
        + [pl.BlockSpec((rows, padded), lambda i: (0, 0))] * count,
        out_specs=[pl.BlockSpec(memory_space=pltpu.VMEM)] * 2,
        compiler_params=pltpu.CompilerParams(vmem_limit_bytes=VMEM),
        cost_estimate=pl.CostEstimate(
            flops=2 * count * rows * D * padded,
            bytes_accessed=2 * count * rows * (D + padded) + 4 * D * unit,
            transcendentals=0,
        ),
    )(jnp.stack([me, s]).astype(jnp.int32), *token_blocks, *grad_blocks)


def spread_kernel(unit, where, blocks, out, held):
    for i in range(blocks.shape[0]):
        held[where[i]] = blocks[i]
    for chip in range(blocks.shape[0]):
        out[:, chip * unit : (chip + 1) * unit] = held[chip]


def widen_kernel(at, gate, up, other_gate, other_up, out):
    for ref, other, low in ((gate, other_gate, 0), (up, other_up, FF)):
        out[at[0], :, low : low + FF] = ref[...].astype(f32)
        out[1 - at[0], :, low : low + FF] = other[...].astype(f32)


def unshuffle_part(terms, order, me):
    half, unit = terms[0].shape[2:]
    (got,) = yield [(CORE, terms[1])]
    total = add(terms[0], got)
    (got,) = yield [("y", total[1].astype(bf16))]
    total = add(total[0], got).astype(bf16)
    blocks, marks = yield from exchange_blocks(total, order)
    mine = whole_call(
        functools.partial(spread_kernel, unit),
        jax.ShapeDtypeStruct((half, FF), bf16),
        [(me ^ f) // 2 for f in marks],
        [blocks],
        scratch=[pltpu.VMEM(blocks.shape, bf16)],
    )
    (other,) = yield [("y", mine)]
    return mine, other


def widen_gate_up(parts, s):
    mine, others = zip(*parts)
    half = mine[0].shape[0]
    whole = whole_call(
        widen_kernel,
        jax.ShapeDtypeStruct((2, half, 2 * FF), f32),
        [s],
        list(mine) + list(others),
    )
    return whole.reshape(2 * half, 2 * FF)


def sum_down(terms, core):
    give = lax.dynamic_index_in_dim(terms, 1 - core, 0, keepdims=False)
    (got,) = yield [(CORE, give)]
    part = add(lax.dynamic_index_in_dim(terms, core, 0, keepdims=False), got).astype(bf16)
    half = part.shape[0] // 2
    (low,) = yield [("y", part[:half])]
    (high,) = yield [("y", part[half:])]
    return add(part, join(low, high))


def rope_tables(positions):
    steps_half = jnp.arange(HD // 2, dtype=f32)
    inverse = rope_base ** (-2.0 * steps_half / HD)
    angles = positions.astype(f32)[:, None] * inverse
    cosines, sines = jnp.cos(angles), jnp.sin(angles)
    return join(cosines, cosines, axis=1), join(-sines, sines, axis=1)


def turn(head, cosines, sines):
    return head * cosines + pltpu.roll(head, HD // 2, 1) * sines


def rms_scale(values):
    return lax.rsqrt(jnp.mean(values * values, axis=-1, keepdims=True) + norm_eps)


def norm_backward(grad_normed, values, gain):
    scale_rows = rms_scale(values)
    scaled = grad_normed * gain
    gain_part = jnp.sum(grad_normed * values * scale_rows, axis=0, keepdims=True)
    grad_values = scale_rows * scaled - values * scale_rows**3 * jnp.mean(
        scaled * values, axis=-1, keepdims=True
    )
    return grad_values, gain_part


def head_at(index):
    return slice(index * HD, (index + 1) * HD)


def masks(second, ids_col, ids_row, other_row):
    shape = (ids_col.shape[0], ids_row.shape[1])
    rows = lax.broadcasted_iota(jnp.int32, shape, 0)
    cols = lax.broadcasted_iota(jnp.int32, shape, 1)
    near = (ids_col[...] == ids_row[...]) & (rows >= cols)
    far = (ids_col[...] == other_row[...]) & (rows + shape[0] * second >= shape[0])
    return near, far


def project_kernel(at, inputs, gain, weight, bias, cosines, sines, normed, queries, kv):
    values = inputs[...].astype(f32)
    rows = (values * rms_scale(values) * gain[...]).astype(bf16)
    normed[...] = rows
    projected = dot(rows, weight[...]) + bias[...]
    cos, sin = cosines[...], sines[...]
    for head in range(HQ):
        queries[:, head_at(head)] = turn(projected[:, head_at(head)], cos, sin).astype(bf16)
    for head in range(KV):
        kv[:, head_at(head)] = turn(projected[:, head_at(HQ + head)], cos, sin).astype(bf16)
    kv[:, KW:] = projected[:, QW + KW :].astype(bf16)


def attend_kernel(
    at, inputs, queries, kv, other, ids_col, ids_row, other_row, weight, gain,
    attended, logs, middle, normed,
):
    near, far = masks(at[0], ids_col, ids_row, other_row)
    factor = HD ** (-0.5)
    lanes = lax.broadcasted_iota(jnp.int32, logs.shape, 1)
    kept = jnp.zeros(logs.shape, f32)
    for head in range(HQ):
        k, v = head_at(head // GROUP), head_at(KV + head // GROUP)
        q = queries[:, head_at(head)]
        first = jnp.where(near, dot_t(q, kv[:, k]) * factor, -1e30)
        second = jnp.where(far, dot_t(q, other[:, k]) * factor, -1e30)
        peak = jnp.maximum(
            jnp.max(first, axis=-1, keepdims=True), jnp.max(second, axis=-1, keepdims=True)
        )
        total = jnp.sum(jnp.exp(first - peak), axis=-1, keepdims=True)
        total = total + jnp.sum(jnp.exp(second - peak), axis=-1, keepdims=True)
        log_total = peak + jnp.log(total)
        kept = jnp.where(lanes == head, log_total, kept)
        out = dot(jnp.exp(first - log_total).astype(bf16), kv[:, v])
        out = out + dot(jnp.exp(second - log_total).astype(bf16), other[:, v])
        attended[:, head_at(head)] = out.astype(bf16)
    logs[...] = kept
    rows = inputs[...].astype(f32) + dot(attended[...], weight[...])
    middle[...] = rows
    normed[...] = (rows * rms_scale(rows) * gain[...]).astype(bf16)


def attend_back_kernel(
    at, grad_normed, middle, gain, cotangent, weight, queries, kv, other,
    ids_col, ids_row, other_row, logs, cosines, sines,
    grad_middle, grad_branch, gain_part, grad_queries, keep, give,
):
    grad_values, part = norm_backward(grad_normed[...], middle[...], gain[...])
    gain_part[...] = part
    grad_rows = cotangent[...].astype(f32) + grad_values
    grad_middle[...] = grad_rows
    branch = grad_rows.astype(bf16)
    grad_branch[...] = branch
    grad_out = dot_t(branch, weight[...]).astype(bf16)
    near, far = masks(at[0], ids_col, ids_row, other_row)
    factor = HD ** (-0.5)
    lanes = lax.broadcasted_iota(jnp.int32, logs.shape, 1)
    cos, sin = cosines[...], -sines[...]
    for group in range(KV):
        k, v = head_at(group), head_at(KV + group)
        sums = [jnp.zeros((kv.shape[0], HD), f32) for _ in range(4)]
        for head in range(group * GROUP, (group + 1) * GROUP):
            q, g = queries[:, head_at(head)], grad_out[:, head_at(head)]
            log_total = jnp.sum(
                jnp.where(lanes == head, logs[...], 0.0), axis=-1, keepdims=True
            )
            first = jnp.where(near, dot_t(q, kv[:, k]) * factor, -1e30)
            second = jnp.where(far, dot_t(q, other[:, k]) * factor, -1e30)
            first, second = jnp.exp(first - log_total), jnp.exp(second - log_total)
            grad_first, grad_second = dot_t(g, kv[:, v]), dot_t(g, other[:, v])
            balance = jnp.sum(first * grad_first, axis=-1, keepdims=True)
            balance = balance + jnp.sum(second * grad_second, axis=-1, keepdims=True)
            grad_first = (first * (grad_first - balance)).astype(bf16)
            grad_second = (second * (grad_second - balance)).astype(bf16)
            grad_q = (dot(grad_first, kv[:, k]) + dot(grad_second, other[:, k])) * factor
            grad_q = turn(grad_q.astype(bf16).astype(f32), cos, sin)
            grad_queries[:, head_at(head)] = grad_q.astype(bf16)
            sums[0] = sums[0] + t_dot(grad_first, q)
            sums[1] = sums[1] + t_dot(first.astype(bf16), g)
            sums[2] = sums[2] + t_dot(grad_second, q)
            sums[3] = sums[3] + t_dot(second.astype(bf16), g)
        keep[:, k] = sums[0] * factor
        keep[:, v] = sums[1]
        give[:, k] = (sums[2] * factor).astype(bf16)
        give[:, v] = sums[3].astype(bf16)


def project_back_kernel(
    at, grad_queries, keep, got, cosines, sines, weight, inputs, gain, grad_middle,
    grad_projected, input_grad, gain_part, bias_part,
):
    grad_kv = (keep[...] + got[...].astype(f32)).astype(bf16)
    cos, sin = cosines[...], -sines[...]
    grad_projected[:, :QW] = grad_queries[...]
    for head in range(KV):
        grad_k = turn(grad_kv[:, head_at(head)].astype(f32), cos, sin)
        grad_projected[:, head_at(HQ + head)] = grad_k.astype(bf16)
    grad_projected[:, QW + KW :] = grad_kv[:, KW:]
    rows = grad_projected[...]
    bias_part[...] = jnp.sum(rows.astype(f32), axis=0, keepdims=True)
    grad_normed = dot_t(rows, weight[...])
    grad_values, part = norm_backward(grad_normed, inputs[...].astype(f32), gain[...])
    gain_part[...] = part
    input_grad[...] = grad_middle[...] + grad_values


def feed_kernel(
    tokens_a, tokens_b, cot_a, cot_b, gate_weight, up_weight, down_weight,
    hidden, grad_gate, grad_up, tokens, cotangent, back_a, back_b, total,
):
    step, steps = pl.program_id(0), pl.num_programs(0)
    half = tokens_a.shape[0]

    @pl.when(step == 0)
    def _():
        tokens[:half], tokens[half:] = tokens_a[...], tokens_b[...]
        cotangent[:half], cotangent[half:] = cot_a[...], cot_b[...]
        total[...] = jnp.zeros_like(total)

    gate = dot(tokens[...], gate_weight[...])
    up = dot(tokens[...], up_weight[...])
    grad_hidden = dot_t(cotangent[...], down_weight[...])
    sigmoid = jax.nn.sigmoid(gate)
    silu = gate * sigmoid
    hidden[...] = (silu * up).astype(bf16)
    gate_rows = (grad_hidden * up * sigmoid * (1.0 + gate * (1.0 - sigmoid))).astype(bf16)
    up_rows = (grad_hidden * silu).astype(bf16)
    grad_gate[...] = gate_rows
    grad_up[...] = up_rows
    total[...] += dot_t(
        join(gate_rows, up_rows, axis=1), join(gate_weight[...], up_weight[...], axis=1)
    )

    @pl.when(step == steps - 1)
    def _():
        back_a[...] = total[:half].astype(back_a.dtype)
        back_b[...] = total[half:].astype(back_b.dtype)


def feed_forward(tokens, cotangent, gate_up_weight, down_weight, back_type):
    half = tokens[0].shape[0]
    if half > 256 and half % 256 == 0:
        parts = [
            feed_forward(
                [v[low : low + 256] for v in tokens],
                [v[low : low + 256] for v in cotangent],
                gate_up_weight,
                down_weight,
                back_type,
            )
            for low in range(0, half, 256)
        ]
        halves = [
            join(*[part[i][low : low + 256] for low in (0, 256) for part in parts])
            for i in range(5)
        ]
        return (*halves, *[join(*[part[i] for part in parts]) for i in (5, 6)])
    rows = 2 * half
    padded = down_weight.shape[0]
    tile = 384
    steps = padded // tile
    whole = pl.BlockSpec((rows, D), lambda j: (0, 0))
    piece = pl.BlockSpec((half, D), lambda j: (0, 0))
    part = pl.BlockSpec((rows, tile), lambda j: (0, j))
    units = jax.ShapeDtypeStruct((rows, padded), bf16)
    lines = jax.ShapeDtypeStruct((rows, D), bf16)
    back = jax.ShapeDtypeStruct((half, D), back_type)
    return pl.pallas_call(
        feed_kernel,
        grid=(steps,),
        out_shape=(units, units, units, lines, lines, back, back),
        in_specs=[piece] * 4
        + [
            pl.BlockSpec((D, tile), lambda j: (0, j)),
            pl.BlockSpec((D, tile), lambda j: (0, j)),
            pl.BlockSpec((tile, D), lambda j: (j, 0)),
        ],
        out_specs=(part, part, part, whole, whole, piece, piece),
        scratch_shapes=[pltpu.VMEM((rows, D), f32)],
        compiler_params=pltpu.CompilerParams(vmem_limit_bytes=VMEM),
        cost_estimate=pl.CostEstimate(
            flops=10 * rows * D * padded,
            bytes_accessed=6 * D * padded + 8 * rows * D + 6 * rows * padded,
            transcendentals=rows * padded,
        ),
    )(*tokens, *cotangent, *gate_up_weight, down_weight)


def pair_kernel(at, own, other, out):
    rows = own.shape[0]
    for core, first, second in ((0, own, other), (1, other, own)):

        @pl.when(at[0] == core)
        def _():
            out[:rows], out[rows : 2 * rows] = first[...], second[...]

    if out.shape[0] > 2 * rows:
        out[2 * rows :] = jnp.zeros((out.shape[0] - 2 * rows, out.shape[1]), out.dtype)


def body(
    inputs,
    positions,
    segments,
    gain_one,
    qkv_weight,
    qkv_bias,
    out_weight,
    gain_two,
    gate_up_weight,
    down_weight,
    cotangent,
):
    tokens = inputs.shape[0] * inputs.shape[1]
    size = lax.axis_size("fsdp")
    me = lax.axis_index("fsdp")
    s = lax.axis_index("seq")
    unit = 2 * FF // size
    padded = -(-unit // 384) * 384

    lanes = Lanes()
    far = far_bits()
    core = me % 2
    input_rows = inputs.reshape(tokens, D)
    grad_rows = cotangent.reshape(tokens, D)
    gate_blocks, up_blocks = split_gate_up(gate_up_weight, me, s)
    cot_blocks, token_blocks = [], []
    qkv = Move(gather_weight(qkv_weight, me, s))
    out = Move(gather_weight_plain(out_weight, me))
    gate = Move(shuffle_part(gate_blocks, [X, *far, Z]))
    up = Move(shuffle_part(up_blocks, [X, *far, Z]))
    cot = Move(gather_tokens(grad_rows, cot_blocks))
    down = Move(swap(CORE, down_weight))
    lanes.round(qkv, (up, 2))
    lanes.round(qkv, (out, 2))
    lanes.round(qkv, gate)
    lanes.round(qkv, out, (gate, 2))
    lanes.round(qkv, out)
    (qkv_full,) = lanes.drain(qkv)

    rows_bf16 = jax.ShapeDtypeStruct((tokens, D), bf16)
    rows_f32 = jax.ShapeDtypeStruct((tokens, D), f32)
    cosines, sines = rope_tables(positions.reshape(tokens))
    ids = segments.reshape(2, tokens)
    ids_row = lax.dynamic_index_in_dim(ids, s, 0)
    other_row = lax.dynamic_index_in_dim(ids, 1 - s, 0)
    ids_col = ids_row.reshape(tokens, 1)
    gain_one, gain_two = gain_one[None], gain_two[None]
    normed, queries, kv = whole_call(
        project_kernel,
        (rows_bf16, rows_bf16, jax.ShapeDtypeStruct((tokens, 2 * KW), bf16)),
        [s],
        [input_rows, gain_one, qkv_full, qkv_bias[None], cosines, sines],
        flops=2 * tokens * D * (QW + 2 * KW),
    )
    lanes.beside(kv)
    other = Move(swap("y", kv))
    lanes.round(other, out, (up, 2), gate)
    other_kv, out_full = lanes.drain(other, out)
    attended, logs, middle, normed_two = whole_call(
        attend_kernel,
        (rows_bf16, jax.ShapeDtypeStruct((tokens, HD), f32), rows_f32, rows_bf16),
        [s],
        [input_rows, queries, kv, other_kv, ids_col, ids_row, other_row, out_full, gain_two],
        flops=2 * tokens * D * (D + 8 * tokens),
    )

    lanes.beside(normed_two)
    token = Move(gather_tokens(normed_two, token_blocks))
    lanes.round(token, gate, up)
    lanes.round(token, (gate, 3), down, (up, 2), (cot, 2))
    lanes.round(cot, up)
    parts = lanes.drain(gate, up)
    gate_full, up_full = [weave_part(*part, me, s) for part in parts]
    (other_down,) = lanes.drain(down)
    down_full = whole_call(
        pair_kernel,
        jax.ShapeDtypeStruct((padded, D), bf16),
        [core],
        [down_weight, other_down],
    )
    lanes.drain(token, cot)
    early = feed_forward(token_blocks[0], cot_blocks[0], (gate_full, up_full), down_full, f32)
    last = feed_forward(
        [after(token_blocks[1][0], early[5]), token_blocks[1][1]],
        cot_blocks[1],
        (gate_full, up_full),
        down_full,
        bf16,
    )
    back = Move(scatter_tokens(early[5:], last[5:]))
    lanes.round(back)

    half = last[5].shape[0]
    gate_terms = gate_up_grad([early[3], last[3]], [early[1], last[1]], me, s)
    out_terms = [[dot(v[0][:half], down_full), dot(v[0][half:], down_full)] for v in (early, last)]
    gate = Move(unshuffle_part(gate_terms, [*far, Z, X], me))
    result = Move(scatter_tokens(out_terms[0], [term.astype(bf16) for term in out_terms[1]]))
    lanes.round(back, gate)
    up_terms = gate_up_grad(
        [early[3], last[3]], [lanes.hold(early[2]), lanes.hold(last[2])], me, s
    )
    up = Move(unshuffle_part(up_terms, [X, Z, *far], me))
    attended_turned = turn_rows(lanes.hold(attended), me, s)
    normed_turned = turn_rows(lanes.hold(normed), me, s)
    lanes.round(back, gate, result, up)
    down_terms = t_dot(lanes.hold(early[0]), early[4]) + t_dot(lanes.hold(last[0]), last[4])
    down_terms = down_terms[:unit].astype(bf16).reshape(2, unit // 2, D)
    down = Move(sum_down(down_terms, core))
    (grad_normed_two,) = lanes.drain(back)
    lanes.round((gate, 2), (up, 2))

    grad_middle, grad_branch, gain_two_part, grad_queries, keep, give = whole_call(
        attend_back_kernel,
        (
            rows_f32,
            rows_bf16,
            jax.ShapeDtypeStruct((1, D), f32),
            rows_bf16,
            jax.ShapeDtypeStruct((tokens, 2 * KW), f32),
            jax.ShapeDtypeStruct((tokens, 2 * KW), bf16),
        ),
        [s],
        [grad_normed_two, middle, gain_two, grad_rows, out_full, queries, kv, other_kv]
        + [ids_col, ids_row, other_row, logs, cosines, sines],
        flops=2 * tokens * D * (D + 20 * tokens),
    )
    other = Move(swap("y", give))
    lanes.more(other)
    (got,) = lanes.drain(other)
    out = Move(scatter_weight(attended_turned, grad_branch, s, 768))
    grad_projected, input_grad, gain_one_part, bias_part = whole_call(
        project_back_kernel,
        (
            jax.ShapeDtypeStruct((tokens, QW + 2 * KW), bf16),
            rows_f32,
            jax.ShapeDtypeStruct((1, D), f32),
            jax.ShapeDtypeStruct((1, QW + 2 * KW), f32),
        ),
        [s],
        [grad_queries, keep, got, cosines, sines, qkv_full, input_rows, gain_one, grad_middle],
        flops=2 * tokens * D * (QW + 2 * KW),
    )
    lanes.beside(grad_projected)
    qkv = Move(scatter_weight(normed_turned, grad_projected, s, 1280))
    sums = Move(sum_everywhere(join(gain_one_part[0], bias_part[0], gain_two_part[0])))
    lanes.round(qkv, down, result)
    lanes.round(down, qkv, out, (result, 2))
    lanes.round(qkv, sums, up, gate)
    lanes.round(qkv, gate, up, down, sums)
    lanes.round(qkv, out, (up, 2), (gate, 2), sums)
    lanes.round(qkv, out, sums)
    lanes.round(out, up, sums)
    qkv_weight_total, out_weight_total, down_total, out_sum, sums, *parts = lanes.drain(
        qkv, out, down, result, sums, gate, up
    )
    gate_up_total = widen_gate_up(parts, s)
    output = (middle + out_sum).astype(bf16).reshape(inputs.shape)
    width = bias_part.shape[1]
    return (
        output,
        input_grad.reshape(inputs.shape),
        sums[:D],
        qkv_weight_total,
        sums[D : D + width],
        out_weight_total,
        sums[D + width :],
        gate_up_total,
        down_total,
    )


def solution(mesh):
    placed = (
        P("fsdp", "seq", None),
        P("fsdp", "seq"),
        P("fsdp", None),
        P(),
        P("fsdp", None),
        P(),
        P("fsdp", None),
        P(),
        P("fsdp", None),
        P("fsdp", None),
        P("fsdp", "seq", None),
    )
    return jax.shard_map(
        body,
        mesh=mesh,
        in_specs=placed,
        out_specs=(
            P("fsdp", "seq", None),
            P("fsdp", "seq", None),
            P(),
            P("fsdp", None),
            P(),
            P("fsdp", None),
            P(),
            P("fsdp", None),
            P("fsdp", None),
        ),
        check_vma=False,
    )
```
